256 devices in a mesh: prompt: 4 (over x), prefix: 8 (over y, core), sample: 8 (over z).
Axes of the slice: x: 4, y: 4, z: 8, core: 2. Of those that a mesh axis runs over, the one named last changes fastest.
Arguments:
- new_hidden: bfloat16 [16, 16, 4, 5120], P('prompt', 'prefix'), may hold values from -6 to 6
- query_projection_weight: bfloat16 [5120, 8192], P(('prompt', 'prefix'), 'sample'), may hold values from -0.078125 to 0.078125
- key_projection_weight: bfloat16 [5120, 1024], P(('prompt', 'prefix'), 'sample'), may hold values from -0.078125 to 0.078125
- value_projection_weight: bfloat16 [5120, 1024], P(('prompt', 'prefix'), 'sample'), may hold values from -0.078125 to 0.078125
- w_out: bfloat16 [8192, 5120], P('sample', ('prompt', 'prefix')), may hold values from -0.0625 to 0.0625
- query_norm_gain: bfloat16 [128], replicated, may hold values from 0.5 to 2
- key_norm_gain: bfloat16 [128], replicated, may hold values from 2 to 8
- prefix_keys: bfloat16 [16, 32768, 8, 128], P('prompt', 'prefix', 'sample'), may hold values from -170 to 170
- prompt_cache_values: bfloat16 [16, 32768, 8, 128], P('prompt', 'prefix', 'sample'), may hold values from -6 to 6
- generated_keys: bfloat16 [16, 16, 512, 8, 128], P('prompt', 'prefix', None, 'sample'), may hold values from -6 to 6
- generated_values: bfloat16 [16, 16, 512, 8, 128], P('prompt', 'prefix', None, 'sample'), may hold values from -6 to 6
- prompt_lengths: int32 [16], P('prompt'), may hold values from 8192 to 32768, as said below
- window_lengths: int32 [16, 16], P('prompt', 'prefix'), may hold values from 1 to 512, as said below
Outputs:
- block_out: bfloat16 [16, 16, 4, 5120], P('prompt', 'prefix', None, 'sample')
The draws below stay inside these ranges and needn't reach their ends.
Inputs may be any that keep to these rules, and one draw needn't show every extreme that they name: `prompt_lengths`: the longest prompt has exactly 32768 tokens. `window_lengths`: some sample's window holds exactly 512 tokens.
All inputs are finite; a program needn't handle non-finite values.
Results may differ from the reference program's by a relative error of at most 0.027.
Values may be sent and summed in bfloat16 or wider, within the bound.
A program may use at most 128 MiB of HBM per device.

```python
import math
import jax
import jax.numpy as jnp
from jax import lax

MODEL_SIZE = 5120
QUERY_HEADS = 64
KEY_VALUE_HEADS = 8
HEAD_SIZE = 128
SAMPLE_COUNT = 16
STEPS = 4
WINDOW_SIZE = 512
PROMPT_COUNT = 16
PROMPT_LENGTH = 32768


def draw_prompt_lengths(key, part):
    key = jax.random.fold_in(key, 11)
    first_key, second_key = jax.random.split(key)
    lengths = jax.random.randint(first_key, (PROMPT_COUNT,), PROMPT_LENGTH // 4, PROMPT_LENGTH + 1)
    longest = jax.random.randint(second_key, (), 0, PROMPT_COUNT)
    return jnp.where(jnp.arange(PROMPT_COUNT) == longest, PROMPT_LENGTH, lengths).astype(jnp.int32)


def draw_window_lengths(key, part):
    key = jax.random.fold_in(key, 17)
    first_key, second_key = jax.random.split(key)
    lengths = jax.random.randint(first_key, (PROMPT_COUNT * SAMPLE_COUNT,), 1, WINDOW_SIZE + 1)
    fullest = jax.random.randint(second_key, (), 0, PROMPT_COUNT * SAMPLE_COUNT)
    lengths = jnp.where(jnp.arange(PROMPT_COUNT * SAMPLE_COUNT) == fullest, WINDOW_SIZE, lengths)
    return lengths.reshape(PROMPT_COUNT, SAMPLE_COUNT).astype(jnp.int32)


def draw_prefix_keys(key, part):
    key = jax.random.fold_in(key, 23)
    fragment_list = jax.random.split(key, 3)
    array_shape = (PROMPT_COUNT, PROMPT_LENGTH, KEY_VALUE_HEADS, HEAD_SIZE)
    row_scaling = jnp.exp(jax.random.uniform(fragment_list[1], (PROMPT_COUNT, PROMPT_LENGTH, KEY_VALUE_HEADS, 1), minval=math.log(0.3), maxval=math.log(3.0)))
    head_scaling = jnp.exp(jax.random.uniform(fragment_list[2], (PROMPT_COUNT, 1, KEY_VALUE_HEADS, 1), minval=math.log(0.3), maxval=math.log(3.0)))
    base = jax.random.truncated_normal(fragment_list[0], -4.0, 4.0, array_shape) * row_scaling * head_scaling
    return base.astype(jnp.bfloat16)


def block_scale(own_key, dims, cuts, least, largest):
    def one(dim, blocks):
        heights = jax.random.uniform(jax.random.fold_in(jax.random.fold_in(own_key, 6), dim), (blocks,), jnp.float32, least / len(cuts), largest / len(cuts))
        return jnp.repeat(jnp.exp(heights), dims[dim] // blocks).reshape((-1,) + (1,) * (len(dims) - dim - 1))

    level = one(*cuts[0])
    for cut in cuts[1:]:
        level = level * one(*cut)
    return level


def gaussian(rng, extent, width, reach, pieces=(), dtype=jnp.bfloat16):
    values = width * jax.random.normal(rng, extent, jnp.float32)
    if pieces:
        values = values * block_scale(rng, extent, pieces, -0.22, 0.18)
    return jnp.clip(values, -reach, reach).astype(dtype)


def setup_inputs(seed: int = 0) -> dict:
    streams_of = jax.random.split(jax.random.key(seed), 14)
    new_hidden = gaussian(streams_of[0], (PROMPT_COUNT, SAMPLE_COUNT, STEPS, MODEL_SIZE), 1.0, 6.0, ((0, 4), (1, 8)))
    query_projection_weight = gaussian(streams_of[1], (MODEL_SIZE, QUERY_HEADS * HEAD_SIZE), MODEL_SIZE ** -0.5, 0.078125, ((0, 32), (1, 8)))
    key_projection_weight = gaussian(streams_of[2], (MODEL_SIZE, KEY_VALUE_HEADS * HEAD_SIZE), MODEL_SIZE ** -0.5, 0.078125, ((0, 32), (1, 8)))
    value_projection_weight = gaussian(streams_of[3], (MODEL_SIZE, KEY_VALUE_HEADS * HEAD_SIZE), MODEL_SIZE ** -0.5, 0.078125, ((0, 32), (1, 8)))
    w_out = gaussian(streams_of[4], (QUERY_HEADS * HEAD_SIZE, MODEL_SIZE), (QUERY_HEADS * HEAD_SIZE) ** -0.5, 0.0625, ((0, 8), (1, 32)))
    query_norm_gain = jnp.clip(jnp.exp(jax.random.uniform(streams_of[5], (HEAD_SIZE,), jnp.float32, math.log(0.5), math.log(2.0))), 0.5, 2.0).astype(jnp.bfloat16)
    key_norm_gain = jnp.clip(jnp.exp(jax.random.uniform(streams_of[6], (HEAD_SIZE,), jnp.float32, math.log(2.0), math.log(8.0))), 2.0, 8.0).astype(jnp.bfloat16)
    prefix_keys = draw_prefix_keys(jax.random.fold_in(streams_of[13], 71), 0)
    prompt_cache_values = gaussian(streams_of[8], (PROMPT_COUNT, PROMPT_LENGTH, KEY_VALUE_HEADS, HEAD_SIZE), 1.0, 6.0, ((0, 4), (1, 8), (2, 8)))
    generated_keys = gaussian(streams_of[9], (PROMPT_COUNT, SAMPLE_COUNT, WINDOW_SIZE, KEY_VALUE_HEADS, HEAD_SIZE), 1.5, 6.0, ((0, 4), (1, 8), (3, 8)))
    generated_values = gaussian(streams_of[10], (PROMPT_COUNT, SAMPLE_COUNT, WINDOW_SIZE, KEY_VALUE_HEADS, HEAD_SIZE), 1.0, 6.0, ((0, 4), (1, 8), (3, 8)))
    prompt_lengths = draw_prompt_lengths(jax.random.fold_in(streams_of[13], 71), 0)
    window_lengths = draw_window_lengths(jax.random.fold_in(streams_of[13], 71), 0)
    return dict(new_hidden=new_hidden, query_projection_weight=query_projection_weight, key_projection_weight=key_projection_weight, value_projection_weight=value_projection_weight, w_out=w_out, query_norm_gain=query_norm_gain, key_norm_gain=key_norm_gain, prefix_keys=prefix_keys, prompt_cache_values=prompt_cache_values, generated_keys=generated_keys, generated_values=generated_values, prompt_lengths=prompt_lengths, window_lengths=window_lengths)


def apply_norm(raw, gain):
    scale = lax.rsqrt(lax.optimization_barrier(jnp.mean(raw * raw, axis=-1, keepdims=True)) + 1e-06)
    return raw * scale * gain.astype(jnp.float32)

def reference(new_hidden, query_projection_weight, key_projection_weight, value_projection_weight, w_out, query_norm_gain, key_norm_gain, prefix_keys, prompt_cache_values, generated_keys, generated_values, prompt_lengths, window_lengths):
    prompt_list, sample_list, decode_step_count, model_width = new_hidden.shape
    query_group_width = QUERY_HEADS // KEY_VALUE_HEADS
    token_matrix = new_hidden.reshape(-1, model_width)
    query_vector = apply_norm(jnp.dot(token_matrix, query_projection_weight, preferred_element_type=jnp.float32).reshape(prompt_list, sample_list, decode_step_count, KEY_VALUE_HEADS, query_group_width, HEAD_SIZE), query_norm_gain).astype(jnp.bfloat16)
    fresh_key = apply_norm(jnp.dot(token_matrix, key_projection_weight, preferred_element_type=jnp.float32).reshape(prompt_list, sample_list, decode_step_count, KEY_VALUE_HEADS, HEAD_SIZE), key_norm_gain).astype(jnp.bfloat16)
    fresh_value = jnp.dot(token_matrix, value_projection_weight, preferred_element_type=jnp.float32).astype(jnp.bfloat16).reshape(prompt_list, sample_list, decode_step_count, KEY_VALUE_HEADS, HEAD_SIZE)
    scale = 1.0 / math.sqrt(HEAD_SIZE)
    causal = jnp.arange(decode_step_count)[None, :] <= jnp.arange(decode_step_count)[:, None]

    def per_head(items):
        q_head, pre_keys, pre_vals, win_keys, win_vals, own_keys, own_vals, length, win_len = items
        q_wide = q_head.astype(jnp.float32)
        pre_scores = jnp.einsum('srgd,nd->srgn', q_wide, pre_keys.astype(jnp.float32)) * scale
        pre_mask = (jnp.arange(pre_keys.shape[0]) < length)[None, None, None, :]
        pre_scores = jnp.where(pre_mask, pre_scores, -1e+30)
        win_scores = jnp.einsum('srgd,swd->srgw', q_wide, win_keys.astype(jnp.float32)) * scale
        win_mask = (jnp.arange(win_keys.shape[1])[None, :] < win_len[:, None])[:, None, None, :]
        win_scores = jnp.where(win_mask, win_scores, -1e+30)
        own_scores = jnp.einsum('srgd,std->srgt', q_wide, own_keys.astype(jnp.float32)) * scale
        own_mask = causal[None, :, None, :]
        own_scores = jnp.where(own_mask, own_scores, -1e+30)
        top = jnp.maximum(lax.optimization_barrier(jnp.max(pre_scores, axis=-1)), jnp.maximum(lax.optimization_barrier(jnp.max(win_scores, axis=-1)), lax.optimization_barrier(jnp.max(own_scores, axis=-1))))
        pre_weight = jnp.where(pre_mask, jnp.exp(pre_scores - top[..., None]), 0.0)
        win_weight = jnp.where(win_mask, jnp.exp(win_scores - top[..., None]), 0.0)
        own_weight = jnp.where(own_mask, jnp.exp(own_scores - top[..., None]), 0.0)
        total = lax.optimization_barrier(jnp.sum(pre_weight, axis=-1)) + lax.optimization_barrier(jnp.sum(win_weight, axis=-1)) + lax.optimization_barrier(jnp.sum(own_weight, axis=-1))
        numer = jnp.einsum('srgn,nd->srgd', pre_weight.astype(jnp.bfloat16).astype(jnp.float32), pre_vals.astype(jnp.float32))
        numer = numer + jnp.einsum('srgw,swd->srgd', win_weight.astype(jnp.bfloat16).astype(jnp.float32), win_vals.astype(jnp.float32))
        numer = numer + jnp.einsum('srgt,std->srgd', own_weight.astype(jnp.bfloat16).astype(jnp.float32), own_vals.astype(jnp.float32))
        return (numer / total[..., None]).astype(jnp.bfloat16)

    def per_prompt(items):
        q_one, pre_keys, pre_vals, win_keys, win_vals, own_keys, own_vals, length, win_len = items
        head_items = (jnp.moveaxis(q_one, 2, 0), jnp.moveaxis(pre_keys, 1, 0), jnp.moveaxis(pre_vals, 1, 0), jnp.moveaxis(win_keys, 2, 0), jnp.moveaxis(win_vals, 2, 0), jnp.moveaxis(own_keys, 2, 0), jnp.moveaxis(own_vals, 2, 0))
        result = lax.map(lambda head_part: per_head(head_part + (length, win_len)), head_items)
        return jnp.moveaxis(result, 0, 2)
    attended = lax.map(per_prompt, (query_vector, prefix_keys, prompt_cache_values, generated_keys, generated_values, fresh_key, fresh_value, prompt_lengths, window_lengths))
    attended = attended.reshape(prompt_list * sample_list * decode_step_count, QUERY_HEADS * HEAD_SIZE)
    block_out = jnp.dot(attended, w_out, preferred_element_type=jnp.float32).astype(jnp.bfloat16)
    return block_out.reshape(prompt_list, sample_list, decode_step_count, model_width)
```

```python
import functools
import math

import jax
import jax.numpy as jnp
from jax import lax
from jax.experimental import pallas as pl
from jax.experimental.pallas import tpu as pltpu
from jax.sharding import PartitionSpec as P

MESH = pl.DeviceIdType.MESH
LOG2E = 1.4426950408889634
NT = (((1,), (1,)), ((), ()))


class Sends:
    def __init__(self, sems):
        self.sems = sems
        self.started = []

    def go(self, src, dst, recv, device):
        copy = pltpu.make_async_remote_copy(
            src_ref=src,
            dst_ref=dst,
            send_sem=self.sems.at[len(self.started)],
            recv_sem=recv,
            device_id=device,
            device_id_type=MESH,
        )
        copy.start()
        self.started.append(copy)

    def finish(self):
        for copy in self.started:
            copy.wait_send()


def arrived(ref, sem):
    pltpu.make_async_copy(ref, ref, sem).wait()


def greet(devices):
    barrier = pltpu.get_barrier_semaphore()
    for device in devices:
        pl.semaphore_signal(barrier, inc=1, device_id=device, device_id_type=MESH)
    pl.semaphore_wait(barrier, len(devices))


def norm(raw, gain):
    scale = lax.rsqrt(jnp.mean(raw * raw, axis=-1, keepdims=True) + 1e-06)
    return raw * scale * gain


def project_kernel(
    px, ny, batch,
    hid, wq, wk, wv, wo, qg, kg,
    q_out, k_out, v_out, wo_out,
    wbuf, tok, acc, part, red, qf, qscr,
    send, loc, w_sem, tw_sem, t_sem, r_sem, q_sem, o_sem, ot_sem,
):
    nn = 2 * ny
    x = lax.axis_index("prompt")
    n = lax.axis_index("prefix")
    y, c = lax.div(n, 2), lax.rem(n, 2)
    right, left = lax.rem(x + 1, px), lax.rem(x + px - 1, px)
    across = lax.rem(x + 2, px)
    rows = hid.shape[0]
    depth = wq.shape[0]
    qcols, kcols = wq.shape[1], wk.shape[1]
    pair = 2 * depth
    window = wbuf.shape[1]
    pad = window - pair
    to_right, to_left = {"prompt": right}, {"prompt": left}
    twin = {"prefix": 2 * y + 1 - c}
    peers = [lax.rem(y + i, ny) for i in range(1, ny)]
    others = [{"prefix": 2 * peer + c} for peer in peers]

    zero = jnp.zeros((px, pad, wbuf.shape[2]), wbuf.dtype)
    wbuf[:, 0:pad, :] = zero
    wbuf[:, pair : pair + pad, :] = zero

    greet([to_right, to_left, twin] + others)
    out = Sends(send)

    base = pl.multiple_of(pad * lax.rem(y, 2) + depth * c, 16)
    mine = pl.ds(base, depth)
    half = depth // 2
    first = pl.ds(base, half)
    second = pl.ds(pl.multiple_of(base + half, 16), half)
    base_t = pl.multiple_of(pad * lax.rem(y, 2) + depth * (1 - c), 16)
    theirs = pl.ds(base_t, depth)
    pieces = ((wq, 0, qcols), (wk, qcols, kcols), (wv, qcols + kcols, kcols))
    for piece, lo, width in pieces:
        spot = wbuf.at[x, mine, lo : lo + width]
        out.go(piece, spot, w_sem.at[0], to_right)
        out.go(piece, spot, w_sem.at[1], to_left)

    def start_of(block, chip):
        return pl.multiple_of(128 * lax.div(pair * ny * block + pair * chip, 128), 128)

    for peer, device in zip(peers, others):
        for block in range(px):
            out.go(
                hid.at[:, pl.ds(start_of(block, peer), window)],
                tok.at[y, block],
                t_sem.at[y],
                device,
            )
    for piece, lo, width in pieces:
        spot = wbuf.at[x, mine, lo : lo + width]
        out.go(piece, spot, tw_sem.at[0], twin)
    for piece, lo, width in pieces:
        spot = wbuf.at[x, mine, lo : lo + width]
        pltpu.make_async_copy(piece, spot, loc.at[0]).start()
    for block in range(px):
        pltpu.make_async_copy(
            hid.at[:, pl.ds(start_of(block, y), window)], tok.at[y, block], loc.at[1]
        ).start()

    orow = pl.ds(pl.multiple_of(depth * c, 16), depth)
    orow_t = pl.ds(pl.multiple_of(depth * (1 - c), 16), depth)
    ofirst = pl.ds(pl.multiple_of(depth * c, 16), half)
    osecond = pl.ds(pl.multiple_of(depth * c + half, 16), half)

    def multiply(block, start):
        lhs = tok[:, block].reshape(ny * rows, window)
        value = jnp.dot(lhs, wbuf[block], preferred_element_type=jnp.float32)
        if start:
            acc[...] = value
        else:
            acc[...] += value

    arrived(wbuf.at[x, mine], loc.at[0])
    arrived(tok.at[y], loc.at[1])
    for peer in peers:
        arrived(tok.at[peer], t_sem.at[peer])
    arrived(wbuf.at[x, theirs], tw_sem.at[0])
    multiply(x, True)

    arrived(wbuf.at[left, mine], w_sem.at[0])
    out.go(wbuf.at[left, first], wbuf.at[left, first], w_sem.at[2], to_right)
    out.go(wbuf.at[left, mine], wbuf.at[left, mine], tw_sem.at[1], twin)
    arrived(wbuf.at[right, mine], w_sem.at[1])
    out.go(wbuf.at[right, second], wbuf.at[right, second], w_sem.at[3], to_left)
    out.go(wbuf.at[right, mine], wbuf.at[right, mine], tw_sem.at[2], twin)

    out.go(wo, wo_out.at[x, orow], o_sem.at[0], to_right)
    out.go(wo, wo_out.at[x, orow], o_sem.at[1], to_left)
    out.go(wo, wo_out.at[x, orow], ot_sem.at[0], twin)
    pltpu.make_async_copy(wo, wo_out.at[x, orow], loc.at[2]).start()

    arrived(wbuf.at[left, theirs], tw_sem.at[1])
    multiply(left, False)
    arrived(wbuf.at[right, theirs], tw_sem.at[2])
    multiply(right, False)
    arrived(wbuf.at[across, first], w_sem.at[2])
    out.go(wbuf.at[across, first], wbuf.at[across, first], tw_sem.at[3], twin)
    arrived(wbuf.at[across, second], w_sem.at[3])
    out.go(wbuf.at[across, second], wbuf.at[across, second], tw_sem.at[4], twin)
    t_first = pl.ds(base_t, half)
    t_second = pl.ds(pl.multiple_of(base_t + half, 16), half)
    arrived(wbuf.at[across, t_first], tw_sem.at[3])
    arrived(wbuf.at[across, t_second], tw_sem.at[4])
    multiply(across, False)

    part[...] = acc[...].astype(part.dtype).reshape(part.shape)
    for peer, device in zip(peers, others):
        out.go(part.at[peer], red.at[y], r_sem.at[y], device)
    red[y] = part[y]
    for peer in peers:
        arrived(red.at[peer], r_sem.at[peer])
    total = red[0].astype(jnp.float32)
    for chip in range(1, ny):
        total = total + red[chip].astype(jnp.float32)

    heads = qcols // 128
    gain = qg[...].astype(jnp.float32)
    for head in range(heads):
        value = norm(total[:, 128 * head : 128 * head + 128], gain)
        for b in range(batch):
            qf[b, 8 * head : 8 * head + 8, :] = value[8 * b : 8 * b + 8]
    qscr[n] = qf[...].astype(qscr.dtype)
    for device in others:
        out.go(qscr.at[n], qscr.at[n], q_sem.at[n], device)
    out.go(qscr.at[n], qscr.at[n], q_sem.at[n], twin)

    keys = norm(total[:, qcols : qcols + kcols], kg[...].astype(jnp.float32))
    values = total[:, qcols + kcols :]
    blank = jnp.zeros((8, 128), jnp.float32)
    for b in range(batch):
        k_out[b] = jnp.concatenate([keys[8 * b : 8 * b + 8], blank], 0).astype(k_out.dtype)
        v_out[b] = jnp.concatenate([values[8 * b : 8 * b + 8], blank], 0).astype(v_out.dtype)

    for peer in peers:
        spot = qscr.at[2 * peer + c]
        arrived(spot, q_sem.at[2 * peer + c])
        out.go(spot, spot, q_sem.at[2 * peer + c], twin)

    arrived(wo_out.at[left, orow], o_sem.at[0])
    out.go(wo_out.at[left, ofirst], wo_out.at[left, ofirst], o_sem.at[2], to_right)
    out.go(wo_out.at[left, orow], wo_out.at[left, orow], ot_sem.at[1], twin)
    arrived(wo_out.at[right, orow], o_sem.at[1])
    out.go(wo_out.at[right, osecond], wo_out.at[right, osecond], o_sem.at[3], to_left)
    out.go(wo_out.at[right, orow], wo_out.at[right, orow], ot_sem.at[2], twin)

    for chip in range(ny):
        spot = qscr.at[2 * chip + 1 - c]
        arrived(spot, q_sem.at[2 * chip + 1 - c])
    q_out[...] = qscr[...]

    arrived(wo_out.at[across, ofirst], o_sem.at[2])
    arrived(wo_out.at[across, osecond], o_sem.at[3])
    out.go(wo_out.at[across, orow], wo_out.at[across, orow], ot_sem.at[3], twin)
    arrived(wo_out.at[x, orow], loc.at[2])
    arrived(wo_out.at[x, orow_t], ot_sem.at[0])
    arrived(wo_out.at[left, orow_t], ot_sem.at[1])
    arrived(wo_out.at[right, orow_t], ot_sem.at[2])
    arrived(wo_out.at[across, orow_t], ot_sem.at[3])
    out.finish()


def project(px, ny, hid, wq, wk, wv, wo, qg, kg, interpret=False):
    nn = 2 * ny
    rows = hid.shape[0]
    batch = rows // 8
    depth = wq.shape[0]
    cols = wq.shape[1] + wk.shape[1] + wv.shape[1]
    heads = wq.shape[1] // 128
    window = 2 * depth + 64
    any_spec = pl.BlockSpec(memory_space=pl.ANY)
    vmem = pl.BlockSpec(memory_space=pltpu.VMEM)
    dma = pltpu.SemaphoreType.DMA
    return pl.pallas_call(
        functools.partial(project_kernel, px, ny, batch),
        out_shape=(
            jax.ShapeDtypeStruct((nn, batch, 8 * heads, 128), jnp.bfloat16),
            jax.ShapeDtypeStruct((batch, 16, 128), jnp.bfloat16),
            jax.ShapeDtypeStruct((batch, 16, 128), jnp.bfloat16),
            jax.ShapeDtypeStruct((px, 2 * depth, wo.shape[1]), jnp.bfloat16),
        ),
        in_specs=[any_spec] * 5 + [vmem] * 2,
        out_specs=(vmem, vmem, vmem, any_spec),
        scratch_shapes=[
            pltpu.VMEM((px, window, cols), jnp.bfloat16),
            pltpu.VMEM((ny, px, rows, window), jnp.bfloat16),
            pltpu.VMEM((ny * rows, cols), jnp.float32),
            pltpu.VMEM((ny, rows, cols), jnp.bfloat16),
            pltpu.VMEM((ny, rows, cols), jnp.bfloat16),
            pltpu.VMEM((batch, 8 * heads, 128), jnp.float32),
            pltpu.VMEM((nn, batch, 8 * heads, 128), jnp.bfloat16),
            dma((80,)),
            dma((3,)),
            dma((4,)),
            dma((5,)),
            dma((ny,)),
            dma((ny,)),
            dma((nn,)),
            dma((4,)),
            dma((4,)),
        ],
        compiler_params=pltpu.CompilerParams(
            collective_id=0, has_side_effects=True, vmem_limit_bytes=48 * 2**20
        ),
        name="project",
    )(hid, wq, wk, wv, wo, qg, kg)


def lanes_of(column, groups):
    shape = (groups * 64, 128)
    row = lax.rem(lax.broadcasted_iota(jnp.int32, shape, 0), 64)
    lane = lax.broadcasted_iota(jnp.int32, shape, 1)
    spread = jnp.where(row == lane, jnp.broadcast_to(column, shape), 0.0)
    return jnp.sum(spread.reshape(groups, 64, 128), axis=1)


def attend_kernel(
    chunk, scale,
    lengths, windows, q_ref, k_ref, v_ref, gk_ref, gv_ref, kn_ref, vn_ref,
    o_ref, l_ref, ow_ref, lw_ref,
):
    b = pl.program_id(0)
    n = lax.axis_index("prefix")
    nn, _, rows, dim = q_ref.shape
    keys_here = k_ref.shape[1]
    rate = scale * LOG2E
    q = q_ref[:, b].reshape(nn * rows, dim)
    valid = lengths[b] - n * keys_here
    top = acc = total = None
    for lo in range(0, keys_here, chunk):
        k = k_ref[0, lo : lo + chunk]
        v = v_ref[0, lo : lo + chunk]
        s = lax.dot_general(q, k, NT, preferred_element_type=jnp.float32)
        at = lo + lax.broadcasted_iota(jnp.int32, (1, chunk), 1)
        s = s + jnp.where(at < valid, 0.0, -1e30)
        here = jnp.max(s, axis=-1, keepdims=True)
        if top is None:
            new = here
        else:
            new = jnp.maximum(top, here)
        w = jnp.exp2((s - new) * rate)
        add = jnp.sum(w, axis=-1, keepdims=True)
        val = jnp.dot(w.astype(jnp.bfloat16), v, preferred_element_type=jnp.float32)
        if top is None:
            total, acc = add, val
        else:
            factor = jnp.exp2((top - new) * rate)
            total, acc = total * factor + add, acc * factor + val
        top = new
    o_ref[:, b] = (acc / total).astype(o_ref.dtype).reshape(nn, rows, dim)
    lse = lanes_of(top * rate + jnp.log2(total), nn)
    for i in range(nn):
        l_ref[i, pl.ds(b, 1), :] = lse[i : i + 1]

    q = q_ref[n, b]
    wide = gk_ref.shape[1]
    s1 = lax.dot_general(q, gk_ref[0], NT, preferred_element_type=jnp.float32)
    s2 = lax.dot_general(q, kn_ref[0], NT, preferred_element_type=jnp.float32)
    row = lax.rem(lax.broadcasted_iota(jnp.int32, (rows, 1), 0), 8)
    sample, step = lax.div(row, 4), lax.rem(row, 4)
    col = lax.broadcasted_iota(jnp.int32, (1, wide), 1)
    whose = (col >= wide // 2).astype(jnp.int32)
    limit = jnp.where(whose == 0, windows[b, 0], windows[b, 1] + wide // 2)
    s1 = jnp.where((whose == sample) & (col < limit), s1, -1e30)
    col = lax.broadcasted_iota(jnp.int32, (1, 16), 1)
    s2 = jnp.where((lax.div(col, 4) == sample) & (lax.rem(col, 4) <= step), s2, -1e30)
    top = jnp.maximum(jnp.max(s1, axis=-1, keepdims=True), jnp.max(s2, axis=-1, keepdims=True))
    w1 = jnp.exp2((s1 - top) * rate)
    w2 = jnp.exp2((s2 - top) * rate)
    total = jnp.sum(w1, axis=-1, keepdims=True) + jnp.sum(w2, axis=-1, keepdims=True)
    acc = jnp.dot(w1.astype(jnp.bfloat16), gv_ref[0], preferred_element_type=jnp.float32)
    acc = acc + jnp.dot(w2.astype(jnp.bfloat16), vn_ref[0], preferred_element_type=jnp.float32)
    ow_ref[b] = acc / total
    lw_ref[pl.ds(b, 1), :] = lanes_of(top * rate + jnp.log2(total), 1)


def attend(lengths, windows, q, keys, values, gen_keys, gen_values, k_new, v_new):
    nn, batch, rows, dim = q.shape
    whole = keys.shape[1]
    wide = gen_keys.shape[1]
    smem = pl.BlockSpec(memory_space=pltpu.SMEM)
    full = lambda shape: pl.BlockSpec(shape, lambda b: (0,) * len(shape))
    each = lambda shape: pl.BlockSpec(shape, lambda b: (b, 0, 0))
    return pl.pallas_call(
        functools.partial(attend_kernel, min(1024, whole), 1.0 / math.sqrt(dim)),
        grid=(batch,),
        out_shape=(
            jax.ShapeDtypeStruct((nn, batch, rows, dim), jnp.bfloat16),
            jax.ShapeDtypeStruct((nn, 8, 128), jnp.float32),
            jax.ShapeDtypeStruct((batch, rows, dim), jnp.float32),
            jax.ShapeDtypeStruct((8, 128), jnp.float32),
        ),
        in_specs=[
            smem,
            smem,
            full((nn, batch, rows, dim)),
            each((1, whole, dim)),
            each((1, whole, dim)),
            each((1, wide, dim)),
            each((1, wide, dim)),
            each((1, 16, dim)),
            each((1, 16, dim)),
        ],
        out_specs=(
            full((nn, batch, rows, dim)),
            full((nn, 8, 128)),
            full((batch, rows, dim)),
            full((8, 128)),
        ),
        compiler_params=pltpu.CompilerParams(vmem_limit_bytes=48 * 2**20),
        name="attend",
    )(lengths, windows, q, keys, values, gen_keys, gen_values, k_new, v_new)


def finish_kernel(
    px, ny, nz, batch,
    o_in, l_in, ow, lw, wo_in,
    out_ref,
    o_rcv, l_rcv, wbuf, attf, att, msg, rcv,
    send, loc, o_sem, l_sem, a_sem, m_sem,
):
    nn = 2 * ny
    x = lax.axis_index("prompt")
    n = lax.axis_index("prefix")
    z = lax.axis_index("sample")
    y, c = lax.div(n, 2), lax.rem(n, 2)
    per = px * nn // nz
    heads = att.shape[2] // 128

    def home(block, chip):
        return lax.div(block * nn + 2 * chip, per)

    first_chip = lax.div(lax.rem(per * z, nn), 2)

    barrier = pltpu.get_barrier_semaphore()
    prefix_peers = [lax.rem(n + i, nn) for i in range(1, nn)]
    for peer in prefix_peers:
        pl.semaphore_signal(barrier, inc=1, device_id={"prefix": peer}, device_id_type=MESH)
    for k in range(2):
        for zz in range(nz):
            chip = first_chip + k

            @pl.when(jnp.logical_or(chip != y, zz != z))
            def _():
                pl.semaphore_signal(
                    barrier,
                    inc=1,
                    device_id={"prefix": 2 * chip + c, "sample": zz},
                    device_id_type=MESH,
                )

    pltpu.make_async_copy(wo_in, wbuf, loc.at[0]).start()
    pltpu.make_async_copy(o_in.at[n], o_rcv.at[n], loc.at[1]).start()
    pltpu.make_async_copy(l_in.at[n], l_rcv.at[n], loc.at[2]).start()
    mine = jnp.int32(0)
    for block in range(px):
        mine = mine + (home(block, y) == z).astype(jnp.int32)
    pl.semaphore_wait(barrier, nn - 1 + px * ny - mine)

    out = Sends(send)
    for peer in prefix_peers:
        device = {"prefix": peer}
        out.go(l_in.at[peer], l_rcv.at[n], l_sem.at[n], device)
        out.go(o_in.at[peer], o_rcv.at[n], o_sem.at[n], device)
    arrived(o_rcv.at[n], loc.at[1])
    arrived(l_rcv.at[n], loc.at[2])
    for peer in prefix_peers:
        arrived(l_rcv.at[peer], l_sem.at[peer])
        arrived(o_rcv.at[peer], o_sem.at[peer])

    own = lw[...]
    top = own
    for i in range(nn):
        top = jnp.maximum(top, l_rcv[i])
    parts = [jnp.exp2(l_rcv[i] - top) for i in range(nn)] + [jnp.exp2(own - top)]
    inverse = 1.0 / sum(parts[1:], parts[0])
    parts = [part * inverse for part in parts]
    row = lax.broadcasted_iota(jnp.int32, (64, 128), 0)
    lane = lax.broadcasted_iota(jnp.int32, (64, 128), 1)
    pick = row == lane
    for b in range(batch):
        total = None
        for i in range(nn + 1):
            weight = jnp.broadcast_to(parts[i][b : b + 1], (64, 128))
            weight = jnp.sum(jnp.where(pick, weight, 0.0), axis=-1, keepdims=True)
            value = ow[b] if i == nn else o_rcv[i, b].astype(jnp.float32)
            total = weight * value if total is None else total + weight * value
        for head in range(heads):
            attf[8 * b : 8 * b + 8, 128 * head : 128 * head + 128] = total[
                8 * head : 8 * head + 8
            ]
    att[y] = attf[...].astype(att.dtype)
    peers = [lax.rem(y + i, ny) for i in range(1, ny)]
    for peer in peers:
        out.go(att.at[y], att.at[y], a_sem.at[y], {"prefix": 2 * peer + c})
    arrived(wbuf, loc.at[0])
    for peer in peers:
        arrived(att.at[peer], a_sem.at[peer])

    odd = lax.rem(y, 2)
    rows = att.shape[1]
    lhs = att[...].reshape(ny * rows, att.shape[2])
    lane = lax.broadcasted_iota(jnp.int32, (16, 128), 1)
    for block in range(px):
        main = wbuf[block, pl.ds(pl.multiple_of(64 * odd, 64), 256), :]
        rest = wbuf[block, pl.ds(pl.multiple_of(256 * (1 - odd), 64), 64), :]
        rest = jnp.concatenate([rest, rest], 0)
        main = lax.dot_general(lhs, main, NT, preferred_element_type=jnp.float32)
        rest = lax.dot_general(lhs, rest, NT, preferred_element_type=jnp.float32)
        for chip in range(ny):
            r = rows * chip
            msg[block, chip, 0:32, :] = main[r : r + 32, 0:128].astype(msg.dtype)
            msg[block, chip, 32:64, :] = main[r : r + 32, 128:256].astype(msg.dtype)
            low, high = rest[r : r + 16], rest[r + 16 : r + 32]
            msg[block, chip, 64:80, :] = jnp.where(lane < 64, low, high).astype(msg.dtype)
        target = home(block, y)
        for i in range(ny):
            chip = lax.rem(y + i, ny)
            copy = pltpu.make_async_remote_copy(
                src_ref=msg.at[block, chip],
                dst_ref=rcv.at[odd, z],
                send_sem=send.at[60 + block * ny + i],
                recv_sem=m_sem.at[odd, z],
                device_id={"prefix": 2 * chip + c, "sample": target},
                device_id_type=MESH,
            )
            if i > 0:
                copy.start()
            else:

                @pl.when(target != z)
                def _():
                    copy.start()

                @pl.when(target == z)
                def _():
                    rcv[odd, z] = msg[block, chip]

    for k in range(2):
        chip = first_chip + k
        for i in range(nz):
            zz = lax.rem(z + i, nz)
            if i > 0:
                arrived(rcv.at[k, zz], m_sem.at[k, zz])
            else:

                @pl.when(chip != y)
                def _():
                    arrived(rcv.at[k, zz], m_sem.at[k, zz])

    sums = []
    for k in range(2):
        total = rcv[k, 0].astype(jnp.float32)
        for zz in range(1, nz):
            total = total + rcv[k, zz].astype(jnp.float32)
        sums.append(total)
    a, d = sums
    out_ref[:, 0:128] = a[0:32].astype(out_ref.dtype)
    out_ref[:, 128:256] = a[32:64].astype(out_ref.dtype)
    a, e = a[64:80], d[64:80]
    low = jnp.where(lane < 64, a, pltpu.roll(e, 64, 1))
    high = jnp.where(lane < 64, pltpu.roll(a, 64, 1), e)
    out_ref[0:16, 256:384] = low.astype(out_ref.dtype)
    out_ref[16:32, 256:384] = high.astype(out_ref.dtype)
    out_ref[:, 384:512] = d[0:32].astype(out_ref.dtype)
    out_ref[:, 512:640] = d[32:64].astype(out_ref.dtype)

    out.finish()
    for block in range(px):
        target = home(block, y)
        for i in range(ny):
            chip = lax.rem(y + i, ny)
            copy = pltpu.make_async_remote_copy(
                src_ref=msg.at[block, chip],
                dst_ref=rcv.at[odd, z],
                send_sem=send.at[60 + block * ny + i],
                recv_sem=m_sem.at[odd, z],
                device_id={"prefix": 2 * chip + c, "sample": target},
                device_id_type=MESH,
            )
            if i > 0:
                copy.wait_send()
            else:

                @pl.when(target != z)
                def _():
                    copy.wait_send()


def finish(px, ny, nz, o, lse, o_win, lse_win, wo):
    nn, batch, rows, dim = o.shape
    tokens = 8 * batch
    width = wo.shape[2]
    any_spec = pl.BlockSpec(memory_space=pl.ANY)
    vmem = pl.BlockSpec(memory_space=pltpu.VMEM)
    dma = pltpu.SemaphoreType.DMA
    return pl.pallas_call(
        functools.partial(finish_kernel, px, ny, nz, batch),
        out_shape=jax.ShapeDtypeStruct((tokens, 640), jnp.bfloat16),
        in_specs=[any_spec, any_spec, vmem, vmem, any_spec],
        out_specs=vmem,
        scratch_shapes=[
            pltpu.VMEM(o.shape, jnp.bfloat16),
            pltpu.VMEM(lse.shape, jnp.float32),
            pltpu.VMEM(wo.shape, jnp.bfloat16),
            pltpu.VMEM((tokens, width), jnp.float32),
            pltpu.VMEM((ny, tokens, width), jnp.bfloat16),
            pltpu.VMEM((px, ny, 80, 128), jnp.bfloat16),
            pltpu.VMEM((2, nz, 80, 128), jnp.bfloat16),
            dma((60 + px * ny,)),
            dma((3,)),
            dma((nn,)),
            dma((nn,)),
            dma((ny,)),
            dma((2, nz)),
        ],
        compiler_params=pltpu.CompilerParams(
            collective_id=1, has_side_effects=True, vmem_limit_bytes=48 * 2**20
        ),
        name="finish",
    )(o, lse, o_win, lse_win, wo)


def on_device(
    px, ny, nz,
    new_hidden, query_projection_weight, key_projection_weight, value_projection_weight, w_out,
    query_norm_gain, key_norm_gain, prefix_keys, prompt_cache_values,
    generated_keys, generated_values, prompt_lengths, window_lengths,
):
    batch, samples, steps, width = new_hidden.shape
    dim = query_norm_gain.shape[0]
    q, k_new, v_new, wo = project(
        px,
        ny,
        new_hidden.reshape(batch * samples * steps, width),
        query_projection_weight,
        key_projection_weight,
        value_projection_weight,
        w_out.T,
        query_norm_gain.reshape(1, dim),
        key_norm_gain.reshape(1, dim),
    )
    o, lse, o_win, lse_win = attend(
        prompt_lengths,
        window_lengths,
        q,
        prefix_keys.reshape(batch, -1, dim),
        prompt_cache_values.reshape(batch, -1, dim),
        generated_keys.reshape(batch, -1, dim),
        generated_values.reshape(batch, -1, dim),
        k_new,
        v_new,
    )
    block = finish(px, ny, nz, o, lse, o_win, lse_win, wo)
    return block.reshape(batch, samples, steps, -1)


def solution(mesh):
    sizes = mesh.shape
    body = functools.partial(
        on_device, sizes["prompt"], sizes["prefix"] // 2, sizes["sample"]
    )
    return jax.shard_map(
        body,
        mesh=mesh,
        in_specs=(
            P("prompt", "prefix", None, None),
            P(("prompt", "prefix"), "sample"),
            P(("prompt", "prefix"), "sample"),
            P(("prompt", "prefix"), "sample"),
            P("sample", ("prompt", "prefix")),
            P(),
            P(),
            P("prompt", "prefix", "sample", None),
            P("prompt", "prefix", "sample", None),
            P("prompt", "prefix", None, "sample", None),
            P("prompt", "prefix", None, "sample", None),
            P("prompt"),
            P("prompt", "prefix"),
        ),
        out_specs=P("prompt", "prefix", None, "sample"),
        check_vma=False,
    )
```

```python
import functools
import math

import jax
import jax.numpy as jnp
from jax import lax
from jax.experimental import pallas as pl
from jax.experimental.pallas import tpu as pltpu
from jax.sharding import PartitionSpec as P

MESH = pl.DeviceIdType.MESH
LOG2E = 1.4426950408889634
NT = (((1,), (1,)), ((), ()))
TN = (((0,), (0,)), ((), ()))
CHUNK = 1024


class Sends:
    def __init__(self, sems):
        self.sems = sems
        self.started = []

    def go(self, src, dst, recv, device, when=None):
        copy = pltpu.make_async_remote_copy(
            src_ref=src,
            dst_ref=dst,
            send_sem=self.sems.at[len(self.started)],
            recv_sem=recv,
            device_id=device,
            device_id_type=MESH,
        )
        if when is None:
            copy.start()
        else:
            pl.when(when)(copy.start)
        self.started.append((copy, when))

    def finish(self):
        for copy, when in self.started:
            if when is None:
                copy.wait_send()
            else:
                pl.when(when)(copy.wait_send)


def arrived(ref, sem):
    pltpu.make_async_copy(ref, ref, sem).wait()


def norm(raw, gain):
    scale = lax.rsqrt(jnp.mean(raw * raw, axis=-1, keepdims=True) + 1e-06)
    return raw * scale * gain


def lanes_of(column, count):
    shape = (count, 128)
    row = lax.broadcasted_iota(jnp.int32, shape, 0)
    lane = lax.broadcasted_iota(jnp.int32, shape, 1)
    spread = jnp.where(row == lane, jnp.broadcast_to(column, shape), 0.0)
    return jnp.sum(spread, axis=0, keepdims=True)


def kernel(
    px, ny, nz,
    lengths, windows, hid, wq, wk, wv, wo, qg, kg, keys, values, gkeys, gvalues,
    out_ref,
    kbuf, vbuf, gkb, gvb, wbuf, obuf, tok, acc, part_a, part_b, red_a, red_b,
    qf, qa, qb, kn, vn, pa, pb, la, lb, ra, rb, sa, sb, ow, lw, attf, att, msg, rcv,
    send, loc, w_sem, tw_sem, t_sem, r_sem, q_sem, o_sem, ot_sem, p_sem, s_sem, a_sem, m_sem,
):
    nn = 2 * ny
    x = lax.axis_index("prompt")
    n = lax.axis_index("prefix")
    z = lax.axis_index("sample")
    y, c = lax.div(n, 2), lax.rem(n, 2)
    odd = lax.rem(y, 2)
    right, left = lax.rem(x + 1, px), lax.rem(x + px - 1, px)
    across = lax.rem(x + 2, px)
    rows, width = hid.shape
    batch = keys.shape[0]
    keys_here = keys.shape[1]
    depth = wq.shape[0]
    qcols, kcols = wq.shape[1], wk.shape[1]
    cols = qcols + 2 * kcols
    cut = qcols // 2
    pair = 2 * depth
    window = wbuf.shape[1]
    pad = window - pair
    heads = qcols // 128
    hh = heads // 2
    gr = 8 * hh
    rate = LOG2E / math.sqrt(128)
    twin = {"prefix": 2 * y + 1 - c}
    peers = [lax.rem(y + i, ny) for i in range(1, ny)]
    others = [{"prefix": 2 * peer + c} for peer in peers]
    prefix_peers = [lax.rem(n + i, nn) for i in range(1, nn)]
    x_targets = [{"prompt": right}, {"prompt": left}, {"prompt": across}]
    x_sources = [left, right, across]
    per = px * nn // nz

    def home(block, chip):
        return lax.div(block * nn + 2 * chip, per)

    first_chip = lax.div(lax.rem(per * z, nn), 2)

    for i, (src, dst) in enumerate(
        ((keys, kbuf), (values, vbuf), (gkeys, gkb), (gvalues, gvb))
    ):
        pltpu.make_async_copy(src, dst, loc.at[3 + i]).start()
    zero = jnp.zeros((px, pad, cols), wbuf.dtype)
    wbuf[:, 0:pad, :] = zero
    wbuf[:, pair : pair + pad, :] = zero

    barrier = pltpu.get_barrier_semaphore()
    greeted = x_targets + [{"prefix": peer} for peer in prefix_peers]
    for device in greeted:
        pl.semaphore_signal(barrier, inc=1, device_id=device, device_id_type=MESH)
    for k in range(2):
        chip = first_chip + k
        for zz in range(nz):

            @pl.when(jnp.logical_or(chip != y, zz != z))
            def _():
                pl.semaphore_signal(
                    barrier,
                    inc=1,
                    device_id={"prefix": 2 * chip + c, "sample": zz},
                    device_id_type=MESH,
                )

    mine_too = jnp.int32(0)
    for block in range(px):
        mine_too = mine_too + (home(block, y) == z).astype(jnp.int32)
    pl.semaphore_wait(barrier, len(greeted) + px * ny - mine_too)

    out = Sends(send)
    base = pl.multiple_of(pad * odd + depth * c, 16)
    mine = pl.ds(base, depth)
    theirs = pl.ds(pl.multiple_of(pad * odd + depth * (1 - c), 16), depth)
    group_a = ((wq.at[:, 0:cut], 0, cut),)
    group_b = (
        (wq.at[:, cut:qcols], cut, qcols - cut),
        (wk, qcols, kcols),
        (wv, qcols + kcols, kcols),
    )
    spans = (slice(0, cut), slice(cut, cols))

    def send_weights(group, which):
        for piece, lo, size in (group_a, group_b)[group]:
            spot = wbuf.at[x, mine, lo : lo + size]
            if which == 3:
                out.go(piece, spot, tw_sem.at[group, 3], twin)
            elif which == 4:
                pltpu.make_async_copy(piece, spot, loc.at[group]).start()
            else:
                out.go(piece, spot, w_sem.at[group, which], x_targets[which])

    def start_of(block, chip):
        return pl.multiple_of(128 * lax.div(pair * ny * block + pair * chip, 128), 128)

    for which in range(3):
        send_weights(0, which)
    for peer, device in zip(peers, others):
        for block in range(px):
            out.go(
                hid.at[:, pl.ds(start_of(block, peer), window)],
                tok.at[y, block],
                t_sem.at[y],
                device,
            )
    send_weights(0, 3)
    send_weights(0, 4)
    for block in range(px):
        pltpu.make_async_copy(
            hid.at[:, pl.ds(start_of(block, y), window)], tok.at[y, block], loc.at[2]
        ).start()
    send_weights(1, 3)
    send_weights(1, 4)

    def multiply(block, group, start):
        span = spans[group]
        lhs = tok[:, block].reshape(ny * rows, window)
        value = jnp.dot(lhs, wbuf[block, :, span], preferred_element_type=jnp.float32)
        if start:
            acc[:, span] = value
        else:
            acc[:, span] += value

    orow = pl.ds(pl.multiple_of(depth * c, 16), depth)
    orow_t = pl.ds(pl.multiple_of(depth * (1 - c), 16), depth)

    def project(group, after):
        span = spans[group]
        arrived(wbuf.at[x, mine, span], loc.at[group])
        if group == 0:
            arrived(tok.at[y], loc.at[2])
            for peer in peers:
                arrived(tok.at[peer], t_sem.at[peer])
        arrived(wbuf.at[x, theirs, span], tw_sem.at[group, 3])
        multiply(x, group, True)
        for which, source in enumerate(x_sources):
            spot = wbuf.at[source, mine, span]
            arrived(spot, w_sem.at[group, which])
            out.go(spot, spot, tw_sem.at[group, which], twin)
            after(which)
        for which, source in enumerate(x_sources):
            arrived(wbuf.at[source, theirs, span], tw_sem.at[group, which])
            multiply(source, group, False)
        part, red = ((part_a, red_a), (part_b, red_b))[group]
        part[...] = acc[:, span].astype(part.dtype).reshape(part.shape)
        for peer, device in zip(peers, others):
            out.go(part.at[peer], red.at[y], r_sem.at[group, y], device)
        red[y] = part[y]

    gain = qg[...].astype(jnp.float32)

    def own(group):
        red = (red_a, red_b)[group]
        for peer in peers:
            arrived(red.at[peer], r_sem.at[group, peer])
        total = red[0].astype(jnp.float32)
        for chip in range(1, ny):
            total = total + red[chip].astype(jnp.float32)
        for head in range(hh):
            value = norm(total[:, 128 * head : 128 * head + 128], gain)
            for b in range(batch):
                qf[b, 8 * head : 8 * head + 8, :] = value[8 * b : 8 * b + 8]
        q = (qa, qb)[group]
        q[n] = qf[...].astype(q.dtype)
        for peer in prefix_peers:
            out.go(q.at[n], q.at[n], q_sem.at[group, n], {"prefix": peer})
        return total

    def queries(group):
        q = (qa, qb)[group]
        for peer in prefix_peers:
            arrived(q.at[peer], q_sem.at[group, peer])

    def attend(b, group, store_lse):
        q = (qa, qb)[group][:, b].reshape(nn * gr, 128)
        valid = lengths[b] - n * keys_here
        top = total = value = None
        for lo in range(0, keys_here, CHUNK):
            size = min(CHUNK, keys_here - lo)
            k = kbuf[b, lo : lo + size]
            v = vbuf[b, lo : lo + size]
            s = lax.dot_general(k, q, NT, preferred_element_type=jnp.float32)
            at = lo + lax.broadcasted_iota(jnp.int32, (size, 1), 0)
            s = s + jnp.where(at < valid, 0.0, -1e30)
            here = jnp.max(s, axis=0, keepdims=True)
            new = here if top is None else jnp.maximum(top, here)
            w = jnp.exp2((s - new) * rate)
            add = jnp.sum(w, axis=0, keepdims=True)
            val = lax.dot_general(
                v, w.astype(jnp.bfloat16), TN, preferred_element_type=jnp.float32
            )
            if top is None:
                total, value = add, val
            else:
                factor = jnp.exp2((top - new) * rate)
                total, value = total * factor + add, value * factor + val
            top = new
        p = (pa, pb)[group]
        p[:, b] = (value / total).T.astype(p.dtype).reshape(nn, gr, 128)
        store_lse(top * rate + jnp.log2(total))

    def attend_own(b):
        q = jnp.concatenate([qa[n, b], qb[n, b]], 0)
        wide = gkb.shape[1]
        s1 = lax.dot_general(q, gkb[b], NT, preferred_element_type=jnp.float32)
        s2 = lax.dot_general(q, kn[b], NT, preferred_element_type=jnp.float32)
        row = lax.rem(lax.broadcasted_iota(jnp.int32, (2 * gr, 1), 0), 8)
        sample, step = lax.div(row, 4), lax.rem(row, 4)
        col = lax.broadcasted_iota(jnp.int32, (1, wide), 1)
        whose = (col >= wide // 2).astype(jnp.int32)
        limit = jnp.where(whose == 0, windows[0, b], windows[1, b] + wide // 2)
        s1 = jnp.where((whose == sample) & (col < limit), s1, -1e30)
        col = lax.broadcasted_iota(jnp.int32, (1, 16), 1)
        s2 = jnp.where((lax.div(col, 4) == sample) & (lax.rem(col, 4) <= step), s2, -1e30)
        top = jnp.maximum(
            jnp.max(s1, axis=-1, keepdims=True), jnp.max(s2, axis=-1, keepdims=True)
        )
        w1 = jnp.exp2((s1 - top) * rate)
        w2 = jnp.exp2((s2 - top) * rate)
        total = jnp.sum(w1, axis=-1, keepdims=True) + jnp.sum(w2, axis=-1, keepdims=True)
        value = jnp.dot(w1.astype(jnp.bfloat16), gvb[b], preferred_element_type=jnp.float32)
        value = value + jnp.dot(
            w2.astype(jnp.bfloat16), vn[b], preferred_element_type=jnp.float32
        )
        ow[b] = value / total
        lse = top * rate + jnp.log2(total)
        lw[0, pl.ds(b, 1), :] = lanes_of(lse[0:gr], gr)
        lw[1, pl.ds(b, 1), :] = lanes_of(lse[gr:], gr)

    project(0, lambda which: send_weights(1, which))
    own(0)

    def send_wo(which):
        out.go(wo, obuf.at[x, orow], o_sem.at[which], x_targets[which])

    project(1, send_wo)
    out.go(wo, obuf.at[x, orow], ot_sem.at[3], twin)
    pltpu.make_async_copy(wo, obuf.at[x, orow], loc.at[7]).start()

    arrived(kbuf, loc.at[3])
    arrived(vbuf, loc.at[4])
    queries(0)

    def attend_a(b, _):
        def store(lse):
            la[pl.ds(b, 1), :] = lse

        attend(b, 0, store)
        return 0

    lax.fori_loop(0, batch // 2, attend_a, 0)

    total = own(1)
    q_there = qcols - cut
    k_new = norm(total[:, q_there : q_there + kcols], kg[...].astype(jnp.float32))
    v_new = total[:, q_there + kcols :]
    blank = jnp.zeros((8, 128), jnp.float32)
    for b in range(batch):
        kn[b] = jnp.concatenate([k_new[8 * b : 8 * b + 8], blank], 0).astype(kn.dtype)
        vn[b] = jnp.concatenate([v_new[8 * b : 8 * b + 8], blank], 0).astype(vn.dtype)

    lax.fori_loop(batch // 2, batch, attend_a, 0)
    for peer in prefix_peers:
        out.go(la, sa.at[n], s_sem.at[0, n], {"prefix": peer})
        out.go(pa.at[peer], ra.at[n], p_sem.at[0, n], {"prefix": peer})
    ra[n] = pa[n]
    sa[n] = la[...]

    arrived(gkb, loc.at[5])
    arrived(gvb, loc.at[6])

    def own_body(b, _):
        attend_own(b)
        return 0

    lax.fori_loop(0, batch, own_body, 0)

    for which, source in enumerate(x_sources):
        spot = obuf.at[source, orow]
        arrived(spot, o_sem.at[which])
        out.go(spot, spot, ot_sem.at[which], twin)

    queries(1)
    half = batch // 2

    def attend_b(h):
        def body(i, _):
            def store(lse):
                lb[h, pl.ds(i, 1), :] = lse

            attend(h * half + i, 1, store)
            return 0

        lax.fori_loop(0, half, body, 0)
        span = slice(h * half, h * half + half)
        for peer in prefix_peers:
            device = {"prefix": peer}
            out.go(lb.at[h], sb.at[n, h], s_sem.at[1 + h, n], device)
            out.go(pb.at[peer, span], rb.at[n, h], p_sem.at[1 + h, n], device)
        rb[n, h] = pb[n, span]
        sb[n, h] = lb[h]

    row = lax.broadcasted_iota(jnp.int32, (gr, 128), 0)
    lane = lax.broadcasted_iota(jnp.int32, (gr, 128), 1)
    pick = row == lane
    many = nn * gr

    def merge(h):
        if h == 0:
            for peer in prefix_peers:
                arrived(sa.at[peer], s_sem.at[0, peer])
                arrived(ra.at[peer], p_sem.at[0, peer])
        for peer in prefix_peers:
            arrived(sb.at[peer, h], s_sem.at[1 + h, peer])
            arrived(rb.at[peer, h], p_sem.at[1 + h, peer])
        shift = lax.rem(many - gr * n, many)
        for group in range(2):
            stats = []
            for i in range(nn):
                s = sa[i] if group == 0 else sb[i, h]
                stats.append(pltpu.roll(s, shift, 1)[:, 0:128])
            lo = half * h if group == 0 else 0
            mine_stats = lw[group, half * h : half * h + half, :]
            stats = [s[lo : lo + half] for s in stats] + [mine_stats]
            top = functools.reduce(jnp.maximum, stats)
            parts = [jnp.exp2(s - top) for s in stats]
            inverse = 1.0 / functools.reduce(lambda u, w: u + w, parts)
            parts = [part * inverse for part in parts]
            for i in range(half):
                b = half * h + i
                total = None
                for source in range(nn + 1):
                    weight = jnp.broadcast_to(parts[source][i : i + 1], (gr, 128))
                    weight = jnp.sum(jnp.where(pick, weight, 0.0), axis=-1, keepdims=True)
                    if source == nn:
                        value = ow[b, gr * group : gr * group + gr]
                    elif group == 0:
                        value = ra[source, b].astype(jnp.float32)
                    else:
                        value = rb[source, h, i].astype(jnp.float32)
                    total = weight * value if total is None else total + weight * value
                for head in range(hh):
                    at = 128 * (hh * group + head)
                    attf[8 * i : 8 * i + 8, at : at + 128] = total[8 * head : 8 * head + 8]
        att[h, y] = attf[...].astype(att.dtype)
        for device in others:
            out.go(att.at[h, y], att.at[h, y], a_sem.at[h, y], device)

    lane8 = lax.broadcasted_iota(jnp.int32, (8, 128), 1)

    def output(h):
        for peer in peers:
            arrived(att.at[h, peer], a_sem.at[h, peer])
        lhs = att[h].reshape(ny * 16, att.shape[3])
        blank = jnp.zeros((8, 128), jnp.float32)
        for block in range(px):
            main = obuf[block, pl.ds(pl.multiple_of(64 * odd, 64), 256), :]
            rest = obuf[block, pl.ds(pl.multiple_of(256 * (1 - odd), 64), 64), :]
            rest = jnp.concatenate([rest, rest], 0)
            main = lax.dot_general(lhs, main, NT, preferred_element_type=jnp.float32)
            rest = lax.dot_general(lhs, rest, NT, preferred_element_type=jnp.float32)
            for chip in range(ny):
                r = 16 * chip
                msg[h, block, chip, 0:16, :] = main[r : r + 16, 0:128].astype(msg.dtype)
                msg[h, block, chip, 16:32, :] = main[r : r + 16, 128:256].astype(msg.dtype)
                tail = jnp.where(lane8 < 64, rest[r : r + 8], rest[r + 8 : r + 16])
                tail = jnp.concatenate([tail, blank], 0)
                msg[h, block, chip, 32:48, :] = tail.astype(msg.dtype)
            target = home(block, y)
            for i in range(ny):
                chip = lax.rem(y + i, ny)
                out.go(
                    msg.at[h, block, chip],
                    rcv.at[h, odd, z],
                    m_sem.at[h, odd, z],
                    {"prefix": 2 * chip + c, "sample": target},
                    None if i > 0 else target != z,
                )

            @pl.when(target == z)
            def _():
                rcv[h, odd, z] = msg[h, block, y]

    def collect(h):
        sums = []
        for k in range(2):
            chip = first_chip + k
            for i in range(nz):
                zz = lax.rem(z + i, nz)
                if i > 0:
                    arrived(rcv.at[h, k, zz], m_sem.at[h, k, zz])
                else:

                    @pl.when(chip != y)
                    def _():
                        arrived(rcv.at[h, k, zz], m_sem.at[h, k, zz])

        for k in range(2):
            total = rcv[h, k, 0].astype(jnp.float32)
            for zz in range(1, nz):
                total = total + rcv[h, k, zz].astype(jnp.float32)
            sums.append(total)
        a, d = sums
        at = slice(16 * h, 16 * h + 16)
        out_ref[at, 0:128] = a[0:16].astype(out_ref.dtype)
        out_ref[at, 128:256] = a[16:32].astype(out_ref.dtype)
        u, e = a[32:40], d[32:40]
        low = jnp.where(lane8 < 64, u, pltpu.roll(e, 64, 1))
        high = jnp.where(lane8 < 64, pltpu.roll(u, 64, 1), e)
        out_ref[at, 256:384] = jnp.concatenate([low, high], 0).astype(out_ref.dtype)
        out_ref[at, 384:512] = d[0:16].astype(out_ref.dtype)
        out_ref[at, 512:640] = d[16:32].astype(out_ref.dtype)

    attend_b(0)
    attend_b(1)
    merge(0)
    arrived(obuf.at[x, orow], loc.at[7])
    for which, source in enumerate(x_sources + [x]):
        arrived(obuf.at[source, orow_t], ot_sem.at[which])
    merge(1)
    output(0)
    output(1)
    collect(0)
    collect(1)
    out.finish()


def block_of(px, ny, nz, lengths, windows, hid, wq, wk, wv, wo, qg, kg, keys, values, gk, gv):
    nn = 2 * ny
    rows = hid.shape[0]
    batch = rows // 8
    half = batch // 2
    depth = wq.shape[0]
    qcols = wq.shape[1]
    cols = qcols + 2 * wk.shape[1]
    cut = qcols // 2
    heads = qcols // 128
    gr = 4 * heads
    window = 2 * depth + 64
    any_spec = pl.BlockSpec(memory_space=pl.ANY)
    vmem = pl.BlockSpec(memory_space=pltpu.VMEM)
    smem = pl.BlockSpec(memory_space=pltpu.SMEM)
    dma = pltpu.SemaphoreType.DMA
    bf = jnp.bfloat16
    f32 = jnp.float32
    scratch = [
        (keys.shape, bf),
        (values.shape, bf),
        (gk.shape, bf),
        (gv.shape, bf),
        ((px, window, cols), bf),
        ((px, 2 * depth, wo.shape[1]), bf),
        ((ny, px, rows, window), bf),
        ((ny * rows, cols), f32),
        ((ny, rows, cut), bf),
        ((ny, rows, cols - cut), bf),
        ((ny, rows, cut), bf),
        ((ny, rows, cols - cut), bf),
        ((batch, gr, 128), f32),
        ((nn, batch, gr, 128), bf),
        ((nn, batch, gr, 128), bf),
        ((batch, 16, 128), bf),
        ((batch, 16, 128), bf),
        ((nn, batch, gr, 128), bf),
        ((nn, batch, gr, 128), bf),
        ((8, nn * gr), f32),
        ((2, 8, nn * gr), f32),
        ((nn, batch, gr, 128), bf),
        ((nn, 2, half, gr, 128), bf),
        ((nn, 8, nn * gr), f32),
        ((nn, 2, 8, nn * gr), f32),
        ((batch, 2 * gr, 128), f32),
        ((2, 8, 128), f32),
        ((16, qcols), f32),
        ((2, ny, 16, qcols), bf),
        ((2, px, ny, 48, 128), bf),
        ((2, 2, nz, 48, 128), bf),
    ]
    return pl.pallas_call(
        functools.partial(kernel, px, ny, nz),
        out_shape=jax.ShapeDtypeStruct((rows, 640), bf),
        in_specs=[smem, smem] + [any_spec] * 5 + [vmem] * 2 + [any_spec] * 4,
        out_specs=vmem,
        scratch_shapes=[pltpu.VMEM(shape, dtype) for shape, dtype in scratch]
        + [
            dma((160,)),
            dma((8,)),
            dma((2, 3)),
            dma((2, 4)),
            dma((ny,)),
            dma((2, ny)),
            dma((2, nn)),
            dma((3,)),
            dma((4,)),
            dma((3, nn)),
            dma((3, nn)),
            dma((2, ny)),
            dma((2, 2, nz)),
        ],
        compiler_params=pltpu.CompilerParams(
            collective_id=0, has_side_effects=True, vmem_limit_bytes=60 * 2**20
        ),
        name="block",
    )(lengths, windows, hid, wq, wk, wv, wo, qg, kg, keys, values, gk, gv)


def on_device(
    px, ny, nz,
    new_hidden, query_projection_weight, key_projection_weight, value_projection_weight, w_out,
    query_norm_gain, key_norm_gain, prefix_keys, prompt_cache_values,
    generated_keys, generated_values, prompt_lengths, window_lengths,
):
    batch, samples, steps, width = new_hidden.shape
    dim = query_norm_gain.shape[0]
    block = block_of(
        px,
        ny,
        nz,
        prompt_lengths,
        window_lengths.T,
        new_hidden.reshape(batch * samples * steps, width),
        query_projection_weight,
        key_projection_weight,
        value_projection_weight,
        w_out.T,
        query_norm_gain.reshape(1, dim),
        key_norm_gain.reshape(1, dim),
        prefix_keys.reshape(batch, -1, dim),
        prompt_cache_values.reshape(batch, -1, dim),
        generated_keys.reshape(batch, -1, dim),
        generated_values.reshape(batch, -1, dim),
    )
    return block.reshape(batch, samples, steps, -1)


def solution(mesh):
    sizes = mesh.shape
    body = functools.partial(
        on_device, sizes["prompt"], sizes["prefix"] // 2, sizes["sample"]
    )
    return jax.shard_map(
        body,
        mesh=mesh,
        in_specs=(
            P("prompt", "prefix", None, None),
            P(("prompt", "prefix"), "sample"),
            P(("prompt", "prefix"), "sample"),
            P(("prompt", "prefix"), "sample"),
            P("sample", ("prompt", "prefix")),
            P(),
            P(),
            P("prompt", "prefix", "sample", None),
            P("prompt", "prefix", "sample", None),
            P("prompt", "prefix", None, "sample", None),
            P("prompt", "prefix", None, "sample", None),
            P("prompt"),
            P("prompt", "prefix"),
        ),
        out_specs=P("prompt", "prefix", None, "sample"),
        check_vma=False,
    )
```

```python
import functools
import math

import jax
import jax.numpy as jnp
from jax import lax
from jax.experimental import pallas as pl
from jax.experimental.pallas import tpu as pltpu
from jax.sharding import PartitionSpec as P

MESH = pl.DeviceIdType.MESH
LOG2E = 1.4426950408889634
NT = (((1,), (1,)), ((), ()))
TN = (((0,), (0,)), ((), ()))
CHUNK = 1024


class Sends:
    def __init__(self, sems):
        self.sems = sems
        self.started = []

    def go(self, src, dst, recv, device, when=None):
        copy = pltpu.make_async_remote_copy(
            src_ref=src,
            dst_ref=dst,
            send_sem=self.sems.at[len(self.started)],
            recv_sem=recv,
            device_id=device,
            device_id_type=MESH,
        )
        if when is None:
            copy.start()
        else:
            pl.when(when)(copy.start)
        self.started.append((copy, when))

    def finish(self):
        for copy, when in self.started:
            if when is None:
                copy.wait_send()
            else:
                pl.when(when)(copy.wait_send)


def arrived(ref, sem):
    pltpu.make_async_copy(ref, ref, sem).wait()


def norm(raw, gain):
    scale = lax.rsqrt(jnp.mean(raw * raw, axis=-1, keepdims=True) + 1e-06)
    return raw * scale * gain


def lanes_of(column, count):
    shape = (count, 128)
    row = lax.broadcasted_iota(jnp.int32, shape, 0)
    lane = lax.broadcasted_iota(jnp.int32, shape, 1)
    spread = jnp.where(row == lane, jnp.broadcast_to(column, shape), 0.0)
    return jnp.sum(spread, axis=0, keepdims=True)


def kernel(
    px, ny, nz,
    lengths, windows, hid, wq, wk, wv, wo, qg, kg, keys, values, gkeys, gvalues,
    out_ref,
    kbuf, vbuf, gkb, gvb, wbuf, obuf, tok, acc, part_a, part_b, red_a, red_b,
    qf, qa, qb, kn, vn, pa, pb, la, lb, ra, rb, sa, sb, ow, lw, attf, att, msg, rcv,
    send, loc, w_sem, tw_sem, t_sem, r_sem, q_sem, o_sem, ot_sem, p_sem, s_sem, a_sem, m_sem,
):
    nn = 2 * ny
    x = lax.axis_index("prompt")
    n = lax.axis_index("prefix")
    z = lax.axis_index("sample")
    y, c = lax.div(n, 2), lax.rem(n, 2)
    odd = lax.rem(y, 2)
    right, left = lax.rem(x + 1, px), lax.rem(x + px - 1, px)
    across = lax.rem(x + 2, px)
    xodd = lax.rem(x, 2)
    partner = lax.rem(x + 1 + xodd * (px - 2), px)
    other = lax.rem(x + px - 1 - xodd * (px - 2), px)
    rows, width = hid.shape
    batch = keys.shape[0]
    keys_here = keys.shape[1]
    depth = wq.shape[0]
    qcols, kcols = wq.shape[1], wk.shape[1]
    cols = qcols + 2 * kcols
    cut = qcols // 2
    pair = 2 * depth
    window = wbuf.shape[1]
    pad = window - pair
    heads = qcols // 128
    hh = heads // 2
    gr = 8 * hh
    twin = {"prefix": 2 * y + 1 - c}
    peers = [lax.rem(y + i, ny) for i in range(1, ny)]
    others = [{"prefix": 2 * peer + c} for peer in peers]
    beyond = [{"prompt": other, "prefix": 2 * chip + c} for chip in [y] + peers]
    prefix_peers = [lax.rem(n + i, nn) for i in range(1, nn)]
    x_targets = [{"prompt": right}, {"prompt": left}, {"prompt": across}]
    x_sources = [left, right, across]
    per = px * nn // nz

    def home(block, chip):
        return lax.div(block * nn + 2 * chip, per)

    first_chip = lax.div(lax.rem(per * z, nn), 2)

    for i, (src, dst) in enumerate(
        ((keys, kbuf), (values, vbuf), (gkeys, gkb), (gvalues, gvb))
    ):
        pltpu.make_async_copy(src, dst, loc.at[3 + i]).start()
    zero = jnp.zeros((2, pad, cols), wbuf.dtype)
    wbuf[:, 0:pad, :] = zero
    wbuf[:, pair : pair + pad, :] = zero

    barrier = pltpu.get_barrier_semaphore()
    greeted = x_targets + [{"prefix": peer} for peer in prefix_peers] + beyond[1:]
    for device in greeted:
        pl.semaphore_signal(barrier, inc=1, device_id=device, device_id_type=MESH)
    for k in range(2):
        chip = first_chip + k
        for zz in range(nz):

            @pl.when(jnp.logical_or(chip != y, zz != z))
            def _():
                pl.semaphore_signal(
                    barrier,
                    inc=1,
                    device_id={"prefix": 2 * chip + c, "sample": zz},
                    device_id_type=MESH,
                )

    mine_too = jnp.int32(0)
    for block in range(px):
        mine_too = mine_too + (home(block, y) == z).astype(jnp.int32)
    pl.semaphore_wait(barrier, len(greeted) + px * ny - mine_too)

    out = Sends(send)
    base = pl.multiple_of(pad * odd + depth * c, 16)
    mine = pl.ds(base, depth)
    theirs = pl.ds(pl.multiple_of(pad * odd + depth * (1 - c), 16), depth)
    group_a = ((wq.at[:, 0:cut], 0, cut),)
    group_b = (
        (wq.at[:, cut:qcols], cut, qcols - cut),
        (wk, qcols, kcols),
        (wv, qcols + kcols, kcols),
    )
    spans = (slice(0, cut), slice(cut, cols))

    def send_weights(group):
        for piece, lo, size in (group_a, group_b)[group]:
            spot = wbuf.at[1, mine, lo : lo + size]
            out.go(piece, spot, w_sem.at[group], {"prompt": partner})
        for piece, lo, size in (group_a, group_b)[group]:
            spot = wbuf.at[0, mine, lo : lo + size]
            out.go(piece, spot, tw_sem.at[group, 0], twin)
            pltpu.make_async_copy(piece, spot, loc.at[group]).start()

    def start_of(block, chip):
        return pl.multiple_of(128 * lax.div(pair * ny * block + pair * chip, 128), 128)

    send_weights(0)
    blocks = ((x, partner), (other, lax.rem(other + 1 + (1 - xodd) * (px - 2), px)))
    for i in range(2):
        for chip, device in zip([y] + peers, ([None] + others, beyond)[i]):
            for j in range(2):
                piece = hid.at[:, pl.ds(start_of(blocks[i][j], chip), window)]
                spot = tok.at[j, i, y]
                if device is None:
                    pltpu.make_async_copy(piece, spot, loc.at[8 + j]).start()
                else:
                    out.go(piece, spot, t_sem.at[j, i, y], device)

    def multiply(block, group):
        lhs = tok[block].reshape(2 * ny * rows, window)
        return jnp.dot(
            lhs, wbuf[block, :, spans[group]], preferred_element_type=jnp.float32
        )

    orow = pl.ds(pl.multiple_of(depth * c, 16), depth)
    orow_t = pl.ds(pl.multiple_of(depth * (1 - c), 16), depth)

    def tokens_of(block):
        arrived(tok.at[block, 0, y], loc.at[8 + block])
        for peer in peers:
            arrived(tok.at[block, 0, peer], t_sem.at[block, 0, peer])
        for chip in [y] + peers:
            arrived(tok.at[block, 1, chip], t_sem.at[block, 1, chip])

    def project(group, after):
        span = spans[group]
        arrived(wbuf.at[1, mine, span], w_sem.at[group])
        out.go(wbuf.at[1, mine, span], wbuf.at[1, mine, span], tw_sem.at[group, 1], twin)
        after()
        arrived(wbuf.at[0, mine, span], loc.at[group])
        arrived(wbuf.at[0, theirs, span], tw_sem.at[group, 0])
        if group == 0:
            tokens_of(0)
            tokens_of(1)
        acc[:, span] = multiply(0, group)
        arrived(wbuf.at[1, theirs, span], tw_sem.at[group, 1])
        part, red = ((part_a, red_a), (part_b, red_b))[group]
        sums = acc[:, span] + multiply(1, group)
        part[...] = sums.astype(part.dtype).reshape(part.shape)
        for peer, device in zip(peers, others):
            out.go(part.at[0, peer], red.at[0, y], r_sem.at[group, 0, y], device)
        for chip, device in zip([y] + peers, beyond):
            out.go(part.at[1, chip], red.at[1, y], r_sem.at[group, 1, y], device)
        red[0, y] = part[0, y]

    gain = qg[...].astype(jnp.float32) * (LOG2E / math.sqrt(128))

    def own(group):
        red = (red_a, red_b)[group]
        for peer in peers:
            arrived(red.at[0, peer], r_sem.at[group, 0, peer])
        for chip in [y] + peers:
            arrived(red.at[1, chip], r_sem.at[group, 1, chip])
        total = red[0, 0].astype(jnp.float32)
        for i in range(1, 2 * ny):
            total = total + red[i // ny, i % ny].astype(jnp.float32)
        for head in range(hh):
            value = norm(total[:, 128 * head : 128 * head + 128], gain)
            for b in range(batch):
                qf[b, 8 * head : 8 * head + 8, :] = value[8 * b : 8 * b + 8]
        q = (qa, qb)[group]
        q[n] = qf[...].astype(q.dtype)
        for peer in prefix_peers:
            out.go(q.at[n], q.at[n], q_sem.at[group, n], {"prefix": peer})
        return total

    def queries(group):
        q = (qa, qb)[group]
        for peer in prefix_peers:
            arrived(q.at[peer], q_sem.at[group, peer])

    def attend(h, group, store_lse):
        for i in range(half):
            b = half * h + i
            q = (qa, qb)[group][:, b].reshape(nn * gr, 128)
            valid = lengths[b] - n * keys_here
            top = total = value = None
            scores = []
            for lo in range(0, keys_here, CHUNK):
                size = min(CHUNK, keys_here - lo)
                k = kbuf[b, lo : lo + size]
                s = lax.dot_general(k, q, NT, preferred_element_type=jnp.float32)
                at = lo + lax.broadcasted_iota(jnp.int32, (size, 1), 0)
                s = s + jnp.where(at < valid, 0.0, -1e30)
                here = jnp.max(s, axis=0, keepdims=True)
                top = here if top is None else jnp.maximum(top, here)
                scores.append(s)
            for s, lo in zip(scores, range(0, keys_here, CHUNK)):
                w = jnp.exp2(s - top)
                add = jnp.sum(w, axis=0, keepdims=True)
                v = vbuf[b, lo : lo + s.shape[0]]
                val = lax.dot_general(
                    v, w.astype(jnp.bfloat16), TN, preferred_element_type=jnp.float32
                )
                total = add if total is None else total + add
                value = val if value is None else value + val
            p = (pa, pb)[group]
            p[:, b] = (value / total).T.astype(p.dtype).reshape(nn, gr, 128)
            store_lse(i, top + jnp.log2(total))

    def attend_own(b):
        q = jnp.concatenate([qa[n, b], qb[n, b]], 0)
        wide = gkb.shape[1]
        s1 = lax.dot_general(q, gkb[b], NT, preferred_element_type=jnp.float32)
        s2 = lax.dot_general(q, kn[b], NT, preferred_element_type=jnp.float32)
        row = lax.rem(lax.broadcasted_iota(jnp.int32, (2 * gr, 1), 0), 8)
        sample, step = lax.div(row, 4), lax.rem(row, 4)
        col = lax.broadcasted_iota(jnp.int32, (1, wide), 1)
        whose = (col >= wide // 2).astype(jnp.int32)
        limit = jnp.where(whose == 0, windows[0, b], windows[1, b] + wide // 2)
        s1 = jnp.where((whose == sample) & (col < limit), s1, -1e30)
        col = lax.broadcasted_iota(jnp.int32, (1, 16), 1)
        s2 = jnp.where((lax.div(col, 4) == sample) & (lax.rem(col, 4) <= step), s2, -1e30)
        top = jnp.maximum(
            jnp.max(s1, axis=-1, keepdims=True), jnp.max(s2, axis=-1, keepdims=True)
        )
        w1 = jnp.exp2(s1 - top)
        w2 = jnp.exp2(s2 - top)
        total = jnp.sum(w1, axis=-1, keepdims=True) + jnp.sum(w2, axis=-1, keepdims=True)
        value = jnp.dot(w1.astype(jnp.bfloat16), gvb[b], preferred_element_type=jnp.float32)
        value = value + jnp.dot(
            w2.astype(jnp.bfloat16), vn[b], preferred_element_type=jnp.float32
        )
        ow[b] = value / total
        lse = top + jnp.log2(total)
        lw[0, pl.ds(b, 1), :] = lanes_of(lse[0:gr], gr)
        lw[1, pl.ds(b, 1), :] = lanes_of(lse[gr:], gr)

    half = batch // 2
    project(0, lambda: send_weights(1))

    def send_wo():
        for which in range(3):
            out.go(wo, obuf.at[x, orow], o_sem.at[which], x_targets[which])
        out.go(wo, obuf.at[x, orow], ot_sem.at[3], twin)
        pltpu.make_async_copy(wo, obuf.at[x, orow], loc.at[7]).start()

    project(1, lambda: None)
    own(0)
    total = own(1)
    send_wo()
    q_there = qcols - cut
    k_new = norm(total[:, q_there : q_there + kcols], kg[...].astype(jnp.float32))
    v_new = total[:, q_there + kcols :]
    blank = jnp.zeros((8, 128), jnp.float32)
    for b in range(batch):
        kn[b] = jnp.concatenate([k_new[8 * b : 8 * b + 8], blank], 0).astype(kn.dtype)
        vn[b] = jnp.concatenate([v_new[8 * b : 8 * b + 8], blank], 0).astype(vn.dtype)

    arrived(kbuf, loc.at[3])
    arrived(vbuf, loc.at[4])
    queries(0)
    for h in range(2):

        def store_a(i, lse):
            la[half * h + i : half * h + i + 1, :] = lse

        attend(h, 0, store_a)
    for peer in prefix_peers:
        out.go(la, sa.at[n], s_sem.at[0, n], {"prefix": peer})
        out.go(pa.at[peer], ra.at[n], p_sem.at[0, n], {"prefix": peer})
    ra[n] = pa[n]
    sa[n] = la[...]

    def attend_b(h):
        def store_b(i, lse):
            lb[h, i : i + 1, :] = lse

        attend(h, 1, store_b)
        span = slice(h * half, h * half + half)
        for peer in prefix_peers:
            device = {"prefix": peer}
            out.go(lb.at[h], sb.at[n, h], s_sem.at[1 + h, n], device)
            out.go(pb.at[peer, span], rb.at[n, h], p_sem.at[1 + h, n], device)
        rb[n, h] = pb[n, span]
        sb[n, h] = lb[h]

    row = lax.broadcasted_iota(jnp.int32, (gr, 128), 0)
    lane = lax.broadcasted_iota(jnp.int32, (gr, 128), 1)
    pick = row == lane
    many = nn * gr

    def merge(h):
        if h == 0:
            for peer in prefix_peers:
                arrived(sa.at[peer], s_sem.at[0, peer])
                arrived(ra.at[peer], p_sem.at[0, peer])
        for peer in prefix_peers:
            arrived(sb.at[peer, h], s_sem.at[1 + h, peer])
            arrived(rb.at[peer, h], p_sem.at[1 + h, peer])
        shift = lax.rem(many - gr * n, many)
        for group in range(2):
            stats = []
            for i in range(nn):
                s = sa[i] if group == 0 else sb[i, h]
                stats.append(pltpu.roll(s, shift, 1)[:, 0:128])
            lo = half * h if group == 0 else 0
            mine_stats = lw[group, half * h : half * h + half, :]
            stats = [s[lo : lo + half] for s in stats] + [mine_stats]
            top = functools.reduce(jnp.maximum, stats)
            parts = [jnp.exp2(s - top) for s in stats]
            inverse = 1.0 / functools.reduce(lambda u, w: u + w, parts)
            parts = [part * inverse for part in parts]
            for i in range(half):
                b = half * h + i
                total = None
                for source in range(nn + 1):
                    weight = jnp.broadcast_to(parts[source][i : i + 1], (gr, 128))
                    weight = jnp.sum(jnp.where(pick, weight, 0.0), axis=-1, keepdims=True)
                    if source == nn:
                        value = ow[b, gr * group : gr * group + gr]
                    elif group == 0:
                        value = ra[source, b].astype(jnp.float32)
                    else:
                        value = rb[source, h, i].astype(jnp.float32)
                    total = weight * value if total is None else total + weight * value
                for head in range(hh):
                    at = 128 * (hh * group + head)
                    attf[8 * i : 8 * i + 8, at : at + 128] = total[8 * head : 8 * head + 8]
        att[h, y] = attf[...].astype(att.dtype)
        for device in others:
            out.go(att.at[h, y], att.at[h, y], a_sem.at[h, y], device)

    lane8 = lax.broadcasted_iota(jnp.int32, (8, 128), 1)

    def output(h):
        for peer in peers:
            arrived(att.at[h, peer], a_sem.at[h, peer])
        lhs = att[h].reshape(ny * 16, att.shape[3])
        blank = jnp.zeros((8, 128), jnp.float32)
        for block in range(px):
            main = obuf[block, pl.ds(pl.multiple_of(64 * odd, 64), 256), :]
            rest = obuf[block, pl.ds(pl.multiple_of(256 * (1 - odd), 64), 64), :]
            rest = jnp.concatenate([rest, rest], 0)
            main = lax.dot_general(lhs, main, NT, preferred_element_type=jnp.float32)
            rest = lax.dot_general(lhs, rest, NT, preferred_element_type=jnp.float32)
            for chip in range(ny):
                r = 16 * chip
                msg[h, block, chip, 0:16, :] = main[r : r + 16, 0:128].astype(msg.dtype)
                msg[h, block, chip, 16:32, :] = main[r : r + 16, 128:256].astype(msg.dtype)
                tail = jnp.where(lane8 < 64, rest[r : r + 8], rest[r + 8 : r + 16])
                tail = jnp.concatenate([tail, blank], 0)
                msg[h, block, chip, 32:48, :] = tail.astype(msg.dtype)
            target = home(block, y)
            for i in range(ny):
                chip = lax.rem(y + i, ny)
                out.go(
                    msg.at[h, block, chip],
                    rcv.at[h, odd, z],
                    m_sem.at[h, odd, z],
                    {"prefix": 2 * chip + c, "sample": target},
                    None if i > 0 else target != z,
                )

            @pl.when(target == z)
            def _():
                rcv[h, odd, z] = msg[h, block, y]

    def collect(h):
        sums = []
        for k in range(2):
            chip = first_chip + k
            for i in range(nz):
                zz = lax.rem(z + i, nz)
                if i > 0:
                    arrived(rcv.at[h, k, zz], m_sem.at[h, k, zz])
                else:

                    @pl.when(chip != y)
                    def _():
                        arrived(rcv.at[h, k, zz], m_sem.at[h, k, zz])

        for k in range(2):
            total = rcv[h, k, 0].astype(jnp.float32)
            for zz in range(1, nz):
                total = total + rcv[h, k, zz].astype(jnp.float32)
            sums.append(total)
        a, d = sums
        at = slice(16 * h, 16 * h + 16)
        out_ref[at, 0:128] = a[0:16].astype(out_ref.dtype)
        out_ref[at, 128:256] = a[16:32].astype(out_ref.dtype)
        u, e = a[32:40], d[32:40]
        low = jnp.where(lane8 < 64, u, pltpu.roll(e, 64, 1))
        high = jnp.where(lane8 < 64, pltpu.roll(u, 64, 1), e)
        out_ref[at, 256:384] = jnp.concatenate([low, high], 0).astype(out_ref.dtype)
        out_ref[at, 384:512] = d[0:16].astype(out_ref.dtype)
        out_ref[at, 512:640] = d[16:32].astype(out_ref.dtype)

    queries(1)
    attend_b(0)

    attend_b(1)
    arrived(gkb, loc.at[5])
    arrived(gvb, loc.at[6])

    def own_body(b, _):
        attend_own(b)
        return 0

    lax.fori_loop(0, batch, own_body, 0)
    merge(0)
    for which, source in enumerate(x_sources):
        spot = obuf.at[source, orow]
        arrived(spot, o_sem.at[which])
        out.go(spot, spot, ot_sem.at[which], twin)
    arrived(obuf.at[x, orow], loc.at[7])
    for which, source in enumerate(x_sources + [x]):
        arrived(obuf.at[source, orow_t], ot_sem.at[which])
    merge(1)
    output(0)
    output(1)
    collect(0)
    collect(1)
    out.finish()


def block_of(px, ny, nz, lengths, windows, hid, wq, wk, wv, wo, qg, kg, keys, values, gk, gv):
    nn = 2 * ny
    rows = hid.shape[0]
    batch = rows // 8
    half = batch // 2
    depth = wq.shape[0]
    qcols = wq.shape[1]
    cols = qcols + 2 * wk.shape[1]
    cut = qcols // 2
    heads = qcols // 128
    gr = 4 * heads
    window = 2 * depth + 64
    any_spec = pl.BlockSpec(memory_space=pl.ANY)
    vmem = pl.BlockSpec(memory_space=pltpu.VMEM)
    smem = pl.BlockSpec(memory_space=pltpu.SMEM)
    dma = pltpu.SemaphoreType.DMA
    bf = jnp.bfloat16
    f32 = jnp.float32
    scratch = [
        (keys.shape, bf),
        (values.shape, bf),
        (gk.shape, bf),
        (gv.shape, bf),
        ((2, window, cols), bf),
        ((px, 2 * depth, wo.shape[1]), bf),
        ((2, 2, ny, rows, window), bf),
        ((2 * ny * rows, cols), f32),
        ((2, ny, rows, cut), bf),
        ((2, ny, rows, cols - cut), bf),
        ((2, ny, rows, cut), bf),
        ((2, ny, rows, cols - cut), bf),
        ((batch, gr, 128), f32),
        ((nn, batch, gr, 128), bf),
        ((nn, batch, gr, 128), bf),
        ((batch, 16, 128), bf),
        ((batch, 16, 128), bf),
        ((nn, batch, gr, 128), bf),
        ((nn, batch, gr, 128), bf),
        ((8, nn * gr), f32),
        ((2, 8, nn * gr), f32),
        ((nn, batch, gr, 128), bf),
        ((nn, 2, half, gr, 128), bf),
        ((nn, 8, nn * gr), f32),
        ((nn, 2, 8, nn * gr), f32),
        ((batch, 2 * gr, 128), f32),
        ((2, 8, 128), f32),
        ((16, qcols), f32),
        ((2, ny, 16, qcols), bf),
        ((2, px, ny, 48, 128), bf),
        ((2, 2, nz, 48, 128), bf),
    ]
    return pl.pallas_call(
        functools.partial(kernel, px, ny, nz),
        out_shape=jax.ShapeDtypeStruct((rows, 640), bf),
        in_specs=[smem, smem] + [any_spec] * 5 + [vmem] * 2 + [any_spec] * 4,
        out_specs=vmem,
        scratch_shapes=[pltpu.VMEM(shape, dtype) for shape, dtype in scratch]
        + [
            dma((144,)),
            dma((10,)),
            dma((2,)),
            dma((2, 2)),
            dma((2, 2, ny)),
            dma((2, 2, ny)),
            dma((2, nn)),
            dma((3,)),
            dma((4,)),
            dma((3, nn)),
            dma((3, nn)),
            dma((2, ny)),
            dma((2, 2, nz)),
        ],
        compiler_params=pltpu.CompilerParams(
            collective_id=0, has_side_effects=True, vmem_limit_bytes=60 * 2**20
        ),
        name="block",
    )(lengths, windows, hid, wq, wk, wv, wo, qg, kg, keys, values, gk, gv)


def on_device(
    px, ny, nz,
    new_hidden, query_projection_weight, key_projection_weight, value_projection_weight, w_out,
    query_norm_gain, key_norm_gain, prefix_keys, prompt_cache_values,
    generated_keys, generated_values, prompt_lengths, window_lengths,
):
    batch, samples, steps, width = new_hidden.shape
    dim = query_norm_gain.shape[0]
    block = block_of(
        px,
        ny,
        nz,
        prompt_lengths,
        window_lengths.T,
        new_hidden.reshape(batch * samples * steps, width),
        query_projection_weight,
        key_projection_weight,
        value_projection_weight,
        w_out.T,
        query_norm_gain.reshape(1, dim),
        key_norm_gain.reshape(1, dim),
        prefix_keys.reshape(batch, -1, dim),
        prompt_cache_values.reshape(batch, -1, dim),
        generated_keys.reshape(batch, -1, dim),
        generated_values.reshape(batch, -1, dim),
    )
    return block.reshape(batch, samples, steps, -1)


def solution(mesh):
    sizes = mesh.shape
    body = functools.partial(
        on_device, sizes["prompt"], sizes["prefix"] // 2, sizes["sample"]
    )
    return jax.shard_map(
        body,
        mesh=mesh,
        in_specs=(
            P("prompt", "prefix", None, None),
            P(("prompt", "prefix"), "sample"),
            P(("prompt", "prefix"), "sample"),
            P(("prompt", "prefix"), "sample"),
            P("sample", ("prompt", "prefix")),
            P(),
            P(),
            P("prompt", "prefix", "sample", None),
            P("prompt", "prefix", "sample", None),
            P("prompt", "prefix", None, "sample", None),
            P("prompt", "prefix", None, "sample", None),
            P("prompt"),
            P("prompt", "prefix"),
        ),
        out_specs=P("prompt", "prefix", None, "sample"),
        check_vma=False,
    )
```

```python
import functools
import math

import jax
import jax.numpy as jnp
from jax import lax
from jax.experimental import pallas as pl
from jax.experimental.pallas import tpu as pltpu
from jax.sharding import PartitionSpec as P

MESH = pl.DeviceIdType.MESH
LOG2E = 1.4426950408889634
NT = (((1,), (1,)), ((), ()))
TN = (((0,), (0,)), ((), ()))
CHUNK = 1024


class Sends:
    def __init__(self, sems, single, ruler):
        self.sems, self.single, self.ruler = sems, single, ruler
        self.totals = [0]
        self.conditional = []

    def go(self, src, dst, recv, device, when=None):
        if when is None:
            size = math.prod(src.shape) * src.dtype.itemsize // 256
            if self.totals[-1] + size > self.ruler.shape[0]:
                self.totals.append(0)
            self.totals[-1] += size
            sem = self.sems.at[len(self.totals) - 1]
        else:
            sem = self.single.at[len(self.conditional)]
        copy = pltpu.make_async_remote_copy(
            src_ref=src,
            dst_ref=dst,
            send_sem=sem,
            recv_sem=recv,
            device_id=device,
            device_id_type=MESH,
        )
        if when is None:
            copy.start()
        else:
            pl.when(when)(copy.start)
            self.conditional.append((copy, when))

    def finish(self):
        for i, total in enumerate(self.totals):
            arrived(self.ruler.at[0:total], self.sems.at[i])
        for copy, when in self.conditional:
            pl.when(when)(copy.wait_send)


def arrived(ref, sem):
    pltpu.make_async_copy(ref, ref, sem).wait()


def norm(raw, gain):
    scale = lax.rsqrt(jnp.mean(raw * raw, axis=-1, keepdims=True) + 1e-06)
    return raw * scale * gain


def lanes_of(column, count):
    shape = (count, 128)
    row = lax.broadcasted_iota(jnp.int32, shape, 0)
    lane = lax.broadcasted_iota(jnp.int32, shape, 1)
    spread = jnp.where(row == lane, jnp.broadcast_to(column, shape), 0.0)
    return jnp.sum(spread, axis=0, keepdims=True)


def kernel(
    px, ny, nz,
    lengths, windows, hid, wq, wk, wv, wo, qg, kg, keys, values, gkeys, gvalues,
    out_ref,
    kbuf, vbuf, gkb, gvb, wbuf, obuf, tok, acc, part_a, part_b, red_a, red_b,
    qf, qa, qb, kn, vn, pa, pb, la, lb, ra, rb, sa, sb, ow, lw, attf, att, msg, rcv, ruler,
    send, single, loc, w_sem, tw_sem, t_sem, r_sem, q_sem, o_sem, ot_sem, p_sem, s_sem, a_sem, m_sem,
):
    nn = 2 * ny
    x = lax.axis_index("prompt")
    n = lax.axis_index("prefix")
    z = lax.axis_index("sample")
    y, c = lax.div(n, 2), lax.rem(n, 2)
    odd = lax.rem(y, 2)
    right, left = lax.rem(x + 1, px), lax.rem(x + px - 1, px)
    across = lax.rem(x + 2, px)
    xodd = lax.rem(x, 2)
    partner = lax.rem(x + 1 + xodd * (px - 2), px)
    other = lax.rem(x + px - 1 - xodd * (px - 2), px)
    rows, width = hid.shape
    batch = keys.shape[0]
    keys_here = keys.shape[1]
    depth = wq.shape[0]
    qcols, kcols = wq.shape[1], wk.shape[1]
    cols = qcols + 2 * kcols
    cut = qcols // 2
    pair = 2 * depth
    window = wbuf.shape[1]
    pad = window - pair
    heads = qcols // 128
    hh = heads // 2
    gr = 8 * hh
    twin = {"prefix": 2 * y + 1 - c}
    peers = [lax.rem(y + i, ny) for i in range(1, ny)]
    others = [{"prefix": 2 * peer + c} for peer in peers]
    beyond = [{"prompt": other, "prefix": 2 * chip + c} for chip in [y] + peers]
    prefix_peers = [lax.rem(n + i, nn) for i in range(1, nn)]
    x_targets = [{"prompt": right}, {"prompt": left}, {"prompt": across}]
    x_sources = [left, right, across]
    per = px * nn // nz

    def home(block, chip):
        return lax.div(block * nn + 2 * chip, per)

    first_chip = lax.div(lax.rem(per * z, nn), 2)

    for i, (src, dst) in enumerate(
        ((keys, kbuf), (values, vbuf), (gkeys, gkb), (gvalues, gvb))
    ):
        pltpu.make_async_copy(src, dst, loc.at[3 + i]).start()
    zero = jnp.zeros((2, pad, cols), wbuf.dtype)
    wbuf[:, 0:pad, :] = zero
    wbuf[:, pair : pair + pad, :] = zero

    barrier = pltpu.get_barrier_semaphore()
    greeted = x_targets + [{"prefix": peer} for peer in prefix_peers] + beyond[1:]
    for device in greeted:
        pl.semaphore_signal(barrier, inc=1, device_id=device, device_id_type=MESH)
    for k in range(2):
        chip = first_chip + k
        for zz in range(nz):

            @pl.when(jnp.logical_or(chip != y, zz != z))
            def _():
                pl.semaphore_signal(
                    barrier,
                    inc=1,
                    device_id={"prefix": 2 * chip + c, "sample": zz},
                    device_id_type=MESH,
                )

    mine_too = jnp.int32(0)
    for block in range(px):
        mine_too = mine_too + (home(block, y) == z).astype(jnp.int32)
    pl.semaphore_wait(barrier, len(greeted) + px * ny - mine_too)

    out = Sends(send, single, ruler)
    base = pl.multiple_of(pad * odd + depth * c, 16)
    mine = pl.ds(base, depth)
    theirs = pl.ds(pl.multiple_of(pad * odd + depth * (1 - c), 16), depth)
    group_a = ((wq.at[:, 0:cut], 0, cut),)
    group_b = (
        (wq.at[:, cut:qcols], cut, qcols - cut),
        (wk, qcols, kcols),
        (wv, qcols + kcols, kcols),
    )
    spans = (slice(0, cut), slice(cut, cols))

    def send_weights(group):
        for piece, lo, size in (group_a, group_b)[group]:
            spot = wbuf.at[1, mine, lo : lo + size]
            out.go(piece, spot, w_sem.at[group], {"prompt": partner})
        for piece, lo, size in (group_a, group_b)[group]:
            spot = wbuf.at[0, mine, lo : lo + size]
            out.go(piece, spot, tw_sem.at[group, 0], twin)
            pltpu.make_async_copy(piece, spot, loc.at[group]).start()

    def start_of(block, chip):
        return pl.multiple_of(128 * lax.div(pair * ny * block + pair * chip, 128), 128)

    send_weights(0)
    blocks = ((x, partner), (other, lax.rem(other + 1 + (1 - xodd) * (px - 2), px)))
    for i in range(2):
        for chip, device in zip([y] + peers, ([None] + others, beyond)[i]):
            for j in range(2):
                piece = hid.at[:, pl.ds(start_of(blocks[i][j], chip), window)]
                spot = tok.at[j, i, y]
                if device is None:
                    pltpu.make_async_copy(piece, spot, t_sem.at[0]).start()
                else:
                    out.go(piece, spot, t_sem.at[0], device)

    def multiply(block, group):
        lhs = tok[block].reshape(2 * ny * rows, window)
        return jnp.dot(
            lhs, wbuf[block, :, spans[group]], preferred_element_type=jnp.float32
        )

    orow = pl.ds(pl.multiple_of(depth * c, 16), depth)
    orow_t = pl.ds(pl.multiple_of(depth * (1 - c), 16), depth)

    def project(group, after):
        span = spans[group]
        arrived(wbuf.at[1, mine, span], w_sem.at[group])
        out.go(wbuf.at[1, mine, span], wbuf.at[1, mine, span], tw_sem.at[group, 1], twin)
        after()
        arrived(wbuf.at[0, mine, span], loc.at[group])
        arrived(wbuf.at[0, theirs, span], tw_sem.at[group, 0])
        if group == 0:
            arrived(tok, t_sem.at[0])
        acc[:, span] = multiply(0, group)
        arrived(wbuf.at[1, theirs, span], tw_sem.at[group, 1])
        part, red = ((part_a, red_a), (part_b, red_b))[group]
        sums = acc[:, span] + multiply(1, group)
        part[...] = sums.astype(part.dtype).reshape(part.shape)
        for peer, device in zip(peers, others):
            out.go(part.at[0, peer], red.at[y], r_sem.at[group], device)
        for chip, device in zip([y] + peers, beyond):
            out.go(part.at[1, chip], red.at[ny + y], r_sem.at[group], device)
        red[y] = part[0, y]

    def gain():
        return qg[...].astype(jnp.float32) * (LOG2E / math.sqrt(128))


    def own(group):
        red = (red_a, red_b)[group]
        arrived(red.at[0 : nn - 1], r_sem.at[group])
        total = red[0].astype(jnp.float32)
        for i in range(1, nn):
            total = total + red[i].astype(jnp.float32)
        for head in range(hh):
            value = norm(total[:, 128 * head : 128 * head + 128], gain())
            for b in range(batch):
                qf[b, 8 * head : 8 * head + 8, :] = value[8 * b : 8 * b + 8]
        q = (qa, qb)[group]
        q[n] = qf[...].astype(q.dtype)
        for peer in prefix_peers:
            out.go(q.at[n], q.at[n], q_sem.at[group], {"prefix": peer})
        return total

    def queries(group):
        q = (qa, qb)[group]
        arrived(q.at[0 : nn - 1], q_sem.at[group])

    def attend(h, group, store_lse):
        for i in range(half):
            b = half * h + i
            q = (qa, qb)[group][:, b].reshape(nn * gr, 128)
            valid = lengths[b] - n * keys_here
            top = total = value = None
            scores = []
            for lo in range(0, keys_here, CHUNK):
                size = min(CHUNK, keys_here - lo)
                k = kbuf[b, lo : lo + size]
                s = lax.dot_general(k, q, NT, preferred_element_type=jnp.float32)
                at = lo + lax.broadcasted_iota(jnp.int32, (size, 1), 0)
                s = s + jnp.where(at < valid, 0.0, -1e30)
                here = jnp.max(s, axis=0, keepdims=True)
                top = here if top is None else jnp.maximum(top, here)
                scores.append(s)
            for s, lo in zip(scores, range(0, keys_here, CHUNK)):
                w = jnp.exp2(s - top)
                add = jnp.sum(w, axis=0, keepdims=True)
                v = vbuf[b, lo : lo + s.shape[0]]
                val = lax.dot_general(
                    v, w.astype(jnp.bfloat16), TN, preferred_element_type=jnp.float32
                )
                total = add if total is None else total + add
                value = val if value is None else value + val
            p = (pa, pb)[group]
            p[:, b] = (value / total).T.astype(p.dtype).reshape(nn, gr, 128)
            store_lse(i, top + jnp.log2(total))

    def attend_own(b):
        q = jnp.concatenate([qa[n, b], qb[n, b]], 0)
        wide = gkb.shape[1]
        s1 = lax.dot_general(q, gkb[b], NT, preferred_element_type=jnp.float32)
        s2 = lax.dot_general(q, kn[b], NT, preferred_element_type=jnp.float32)
        row = lax.rem(lax.broadcasted_iota(jnp.int32, (2 * gr, 1), 0), 8)
        sample, step = lax.div(row, 4), lax.rem(row, 4)
        col = lax.broadcasted_iota(jnp.int32, (1, wide), 1)
        whose = (col >= wide // 2).astype(jnp.int32)
        limit = jnp.where(whose == 0, windows[0, b], windows[1, b] + wide // 2)
        s1 = jnp.where((whose == sample) & (col < limit), s1, -1e30)
        col = lax.broadcasted_iota(jnp.int32, (1, 16), 1)
        s2 = jnp.where((lax.div(col, 4) == sample) & (lax.rem(col, 4) <= step), s2, -1e30)
        top = jnp.maximum(
            jnp.max(s1, axis=-1, keepdims=True), jnp.max(s2, axis=-1, keepdims=True)
        )
        w1 = jnp.exp2(s1 - top)
        w2 = jnp.exp2(s2 - top)
        total = jnp.sum(w1, axis=-1, keepdims=True) + jnp.sum(w2, axis=-1, keepdims=True)
        value = jnp.dot(w1.astype(jnp.bfloat16), gvb[b], preferred_element_type=jnp.float32)
        value = value + jnp.dot(
            w2.astype(jnp.bfloat16), vn[b], preferred_element_type=jnp.float32
        )
        ow[b] = value / total
        lse = top + jnp.log2(total)
        lw[0, pl.ds(b, 1), :] = lanes_of(lse[0:gr], gr)
        lw[1, pl.ds(b, 1), :] = lanes_of(lse[gr:], gr)

    half = batch // 2
    project(0, lambda: send_weights(1))

    def send_wo():
        for which in range(3):
            out.go(wo, obuf.at[x, orow], o_sem.at[0], x_targets[which])
        out.go(wo, obuf.at[x, orow], ot_sem.at[0], twin)
        pltpu.make_async_copy(wo, obuf.at[x, orow], loc.at[2]).start()

    project(1, lambda: None)
    own(0)
    total = own(1)
    send_wo()
    q_there = qcols - cut
    k_new = norm(total[:, q_there : q_there + kcols], kg[...].astype(jnp.float32))
    v_new = total[:, q_there + kcols :]
    blank = jnp.zeros((8, 128), jnp.float32)
    for b in range(batch):
        kn[b] = jnp.concatenate([k_new[8 * b : 8 * b + 8], blank], 0).astype(kn.dtype)
        vn[b] = jnp.concatenate([v_new[8 * b : 8 * b + 8], blank], 0).astype(vn.dtype)

    arrived(kbuf, loc.at[3])
    arrived(vbuf, loc.at[4])
    queries(0)
    for h in range(2):

        def store_a(i, lse):
            la[half * h + i : half * h + i + 1, :] = lse

        attend(h, 0, store_a)
    for peer in prefix_peers:
        out.go(la, sa.at[n], s_sem.at[0], {"prefix": peer})
        out.go(pa.at[peer], ra.at[n], p_sem.at[0], {"prefix": peer})
    ra[n] = pa[n]
    sa[n] = la[...]

    def attend_b(h):
        def store_b(i, lse):
            lb[h, i : i + 1, :] = lse

        attend(h, 1, store_b)
        span = slice(h * half, h * half + half)
        for peer in prefix_peers:
            device = {"prefix": peer}
            out.go(lb.at[h], sb.at[n, h], s_sem.at[1 + h], device)
            out.go(pb.at[peer, span], rb.at[n, h], p_sem.at[1 + h], device)
        rb[n, h] = pb[n, span]
        sb[n, h] = lb[h]

    row = lax.broadcasted_iota(jnp.int32, (gr, 128), 0)
    lane = lax.broadcasted_iota(jnp.int32, (gr, 128), 1)
    pick = row == lane
    many = nn * gr

    def merge(h):
        if h == 0:
            arrived(sa.at[0 : nn - 1], s_sem.at[0])
            arrived(ra.at[0 : nn - 1], p_sem.at[0])
        arrived(sb.at[0 : nn - 1, h], s_sem.at[1 + h])
        arrived(rb.at[0 : nn - 1, h], p_sem.at[1 + h])
        shift = lax.rem(many - gr * n, many)
        for group in range(2):
            stats = []
            for i in range(nn):
                s = sa[i] if group == 0 else sb[i, h]
                stats.append(pltpu.roll(s, shift, 1)[:, 0:128])
            lo = half * h if group == 0 else 0
            mine_stats = lw[group, half * h : half * h + half, :]
            stats = [s[lo : lo + half] for s in stats] + [mine_stats]
            top = functools.reduce(jnp.maximum, stats)
            parts = [jnp.exp2(s - top) for s in stats]
            inverse = 1.0 / functools.reduce(lambda u, w: u + w, parts)
            parts = [part * inverse for part in parts]
            for i in range(half):
                b = half * h + i
                total = None
                for source in range(nn + 1):
                    weight = jnp.broadcast_to(parts[source][i : i + 1], (gr, 128))
                    weight = jnp.sum(jnp.where(pick, weight, 0.0), axis=-1, keepdims=True)
                    if source == nn:
                        value = ow[b, gr * group : gr * group + gr]
                    elif group == 0:
                        value = ra[source, b].astype(jnp.float32)
                    else:
                        value = rb[source, h, i].astype(jnp.float32)
                    total = weight * value if total is None else total + weight * value
                for head in range(hh):
                    at = 128 * (hh * group + head)
                    attf[8 * i : 8 * i + 8, at : at + 128] = total[8 * head : 8 * head + 8]
        att[h, y] = attf[...].astype(att.dtype)
        for device in others:
            out.go(att.at[h, y], att.at[h, y], a_sem.at[h], device)

    lane8 = lax.broadcasted_iota(jnp.int32, (8, 128), 1)

    def output(h):
        arrived(att.at[h, 0 : ny - 1], a_sem.at[h])
        lhs = att[h].reshape(ny * 16, att.shape[3])
        blank = jnp.zeros((8, 128), jnp.float32)
        for block in range(px):
            main = obuf[block, pl.ds(pl.multiple_of(64 * odd, 64), 256), :]
            rest = obuf[block, pl.ds(pl.multiple_of(256 * (1 - odd), 64), 64), :]
            rest = jnp.concatenate([rest, rest], 0)
            main = lax.dot_general(lhs, main, NT, preferred_element_type=jnp.float32)
            rest = lax.dot_general(lhs, rest, NT, preferred_element_type=jnp.float32)
            for chip in range(ny):
                r = 16 * chip
                msg[h, block, chip, 0:16, :] = main[r : r + 16, 0:128].astype(msg.dtype)
                msg[h, block, chip, 16:32, :] = main[r : r + 16, 128:256].astype(msg.dtype)
                tail = jnp.where(lane8 < 64, rest[r : r + 8], rest[r + 8 : r + 16])
                tail = jnp.concatenate([tail, blank], 0)
                msg[h, block, chip, 32:48, :] = tail.astype(msg.dtype)
            target = home(block, y)
            for i in range(ny):
                chip = lax.rem(y + i, ny)
                out.go(
                    msg.at[h, block, chip],
                    rcv.at[h, odd * nz + z],
                    m_sem.at[h],
                    {"prefix": 2 * chip + c, "sample": target},
                    None if i > 0 else target != z,
                )

            @pl.when(target == z)
            def _():
                rcv[h, odd * nz + z] = msg[h, block, y]

    def collect(h):
        sums = []
        here = jnp.logical_or(first_chip == y, first_chip + 1 == y)

        @pl.when(here)
        def _():
            arrived(rcv.at[h, 0 : 2 * nz - 1], m_sem.at[h])

        @pl.when(jnp.logical_not(here))
        def _():
            arrived(rcv.at[h], m_sem.at[h])

        for k in range(2):
            total = rcv[h, k * nz].astype(jnp.float32)
            for zz in range(1, nz):
                total = total + rcv[h, k * nz + zz].astype(jnp.float32)
            sums.append(total)
        a, d = sums
        u, e = a[32:40], d[32:40]
        low = jnp.where(lane8 < 64, u, pltpu.roll(e, 64, 1))
        high = jnp.where(lane8 < 64, pltpu.roll(u, 64, 1), e)
        middle = jnp.concatenate([low, high], 0)
        tiles = (a[0:16], a[16:32], middle, d[0:16], d[16:32])
        for j, tile in enumerate(tiles):
            tile = tile.astype(out_ref.dtype)
            for i in range(4):
                out_ref[4 * h + i, :, 128 * j : 128 * j + 128] = tile[4 * i : 4 * i + 4]

    queries(1)
    attend_b(0)

    attend_b(1)
    arrived(gkb, loc.at[5])
    arrived(gvb, loc.at[6])

    def own_body(b, _):
        attend_own(b)
        return 0

    lax.fori_loop(0, batch, own_body, 0)
    merge(0)
    arrived(obuf.at[0 : px - 1, orow], o_sem.at[0])
    for source in x_sources:
        spot = obuf.at[source, orow]
        out.go(spot, spot, ot_sem.at[0], twin)
    arrived(obuf.at[x, orow], loc.at[2])
    arrived(obuf.at[:, orow_t], ot_sem.at[0])
    merge(1)
    output(0)
    output(1)
    collect(0)
    collect(1)
    out.finish()


def block_of(px, ny, nz, lengths, windows, hid, wq, wk, wv, wo, qg, kg, keys, values, gk, gv):
    nn = 2 * ny
    rows = hid.shape[0]
    batch = rows // 8
    half = batch // 2
    depth = wq.shape[0]
    qcols = wq.shape[1]
    cols = qcols + 2 * wk.shape[1]
    cut = qcols // 2
    heads = qcols // 128
    gr = 4 * heads
    window = 2 * depth + 64
    any_spec = pl.BlockSpec(memory_space=pl.ANY)
    vmem = pl.BlockSpec(memory_space=pltpu.VMEM)
    smem = pl.BlockSpec(memory_space=pltpu.SMEM)
    dma = pltpu.SemaphoreType.DMA
    bf = jnp.bfloat16
    f32 = jnp.float32
    scratch = [
        (keys.shape, bf),
        (values.shape, bf),
        (gk.shape, bf),
        (gv.shape, bf),
        ((2, window, cols), bf),
        ((px, 2 * depth, wo.shape[1]), bf),
        ((2, 2, ny, rows, window), bf),
        ((2 * ny * rows, cols), f32),
        ((2, ny, rows, cut), bf),
        ((2, ny, rows, cols - cut), bf),
        ((nn, rows, cut), bf),
        ((nn, rows, cols - cut), bf),
        ((batch, gr, 128), f32),
        ((nn, batch, gr, 128), bf),
        ((nn, batch, gr, 128), bf),
        ((batch, 16, 128), bf),
        ((batch, 16, 128), bf),
        ((nn, batch, gr, 128), bf),
        ((nn, batch, gr, 128), bf),
        ((8, nn * gr), f32),
        ((2, 8, nn * gr), f32),
        ((nn, batch, gr, 128), bf),
        ((nn, 2, half, gr, 128), bf),
        ((nn, 8, nn * gr), f32),
        ((nn, 2, 8, nn * gr), f32),
        ((batch, 2 * gr, 128), f32),
        ((2, 8, 128), f32),
        ((16, qcols), f32),
        ((2, ny, 16, qcols), bf),
        ((2, px, ny, 48, 128), bf),
        ((2, 2 * nz, 48, 128), bf),
        ((4096, 128), bf),
    ]
    return pl.pallas_call(
        functools.partial(kernel, px, ny, nz),
        out_shape=jax.ShapeDtypeStruct((rows // 4, 4, 640), bf),
        in_specs=[smem, smem] + [any_spec] * 5 + [vmem] * 2 + [any_spec] * 4,
        out_specs=vmem,
        scratch_shapes=[pltpu.VMEM(shape, dtype) for shape, dtype in scratch]
        + [
            dma((10,)),
            dma((2 * px,)),
            dma((7,)),
            dma((2,)),
            dma((2, 2)),
            dma((1,)),
            dma((2,)),
            dma((2,)),
            dma((1,)),
            dma((1,)),
            dma((3,)),
            dma((3,)),
            dma((2,)),
            dma((2,)),
        ],
        compiler_params=pltpu.CompilerParams(
            collective_id=0, has_side_effects=True, vmem_limit_bytes=60 * 2**20
        ),
        name="block",
    )(lengths, windows, hid, wq, wk, wv, wo, qg, kg, keys, values, gk, gv)


def on_device(
    px, ny, nz,
    new_hidden, query_projection_weight, key_projection_weight, value_projection_weight, w_out,
    query_norm_gain, key_norm_gain, prefix_keys, prompt_cache_values,
    generated_keys, generated_values, prompt_lengths, window_lengths,
):
    batch, samples, steps, width = new_hidden.shape
    dim = query_norm_gain.shape[0]
    block = block_of(
        px,
        ny,
        nz,
        prompt_lengths,
        window_lengths.T,
        new_hidden.reshape(batch * samples * steps, width),
        query_projection_weight,
        key_projection_weight,
        value_projection_weight,
        w_out.T,
        query_norm_gain.reshape(1, dim),
        key_norm_gain.reshape(1, dim),
        prefix_keys.reshape(batch, -1, dim),
        prompt_cache_values.reshape(batch, -1, dim),
        generated_keys.reshape(batch, -1, dim),
        generated_values.reshape(batch, -1, dim),
    )
    return block.reshape(batch, samples, steps, -1)


def solution(mesh):
    sizes = mesh.shape
    body = functools.partial(
        on_device, sizes["prompt"], sizes["prefix"] // 2, sizes["sample"]
    )
    return jax.shard_map(
        body,
        mesh=mesh,
        in_specs=(
            P("prompt", "prefix", None, None),
            P(("prompt", "prefix"), "sample"),
            P(("prompt", "prefix"), "sample"),
            P(("prompt", "prefix"), "sample"),
            P("sample", ("prompt", "prefix")),
            P(),
            P(),
            P("prompt", "prefix", "sample", None),
            P("prompt", "prefix", "sample", None),
            P("prompt", "prefix", None, "sample", None),
            P("prompt", "prefix", None, "sample", None),
            P("prompt"),
            P("prompt", "prefix"),
        ),
        out_specs=P("prompt", "prefix", None, "sample"),
        check_vma=False,
    )
```

```python
import functools
import math

import jax
import jax.numpy as jnp
from jax import lax
from jax.experimental import pallas as pl
from jax.experimental.pallas import tpu as pltpu
from jax.sharding import PartitionSpec as P

MESH = pl.DeviceIdType.MESH
LOG2E = 1.4426950408889634
NT = (((1,), (1,)), ((), ()))
TN = (((0,), (0,)), ((), ()))
CHUNK = 1024


class Sends:
    def __init__(self, sems, single, ruler):
        self.sems, self.single, self.ruler = sems, single, ruler
        self.totals = [0]
        self.conditional = []

    def go(self, src, dst, recv, device, when=None):
        if when is None:
            size = math.prod(src.shape) * src.dtype.itemsize // 256
            if self.totals[-1] + size > self.ruler.shape[0]:
                self.totals.append(0)
            self.totals[-1] += size
            sem = self.sems.at[len(self.totals) - 1]
        else:
            sem = self.single.at[len(self.conditional)]
        copy = pltpu.make_async_remote_copy(
            src_ref=src,
            dst_ref=dst,
            send_sem=sem,
            recv_sem=recv,
            device_id=device,
            device_id_type=MESH,
        )
        if when is None:
            copy.start()
        else:
            pl.when(when)(copy.start)
            self.conditional.append((copy, when))

    def finish(self):
        for i, total in enumerate(self.totals):
            arrived(self.ruler.at[0:total], self.sems.at[i])
        for copy, when in self.conditional:
            pl.when(when)(copy.wait_send)


def arrived(ref, sem):
    pltpu.make_async_copy(ref, ref, sem).wait()


def norm(raw, gain):
    scale = lax.rsqrt(jnp.mean(raw * raw, axis=-1, keepdims=True) + 1e-06)
    return raw * scale * gain


def lanes_of(column, count):
    shape = (count, 128)
    row = lax.broadcasted_iota(jnp.int32, shape, 0)
    lane = lax.broadcasted_iota(jnp.int32, shape, 1)
    spread = jnp.where(row == lane, jnp.broadcast_to(column, shape), 0.0)
    return jnp.sum(spread, axis=0, keepdims=True)


def kernel(
    px, ny, nz,
    lengths, windows, hid, wq, wk, wv, wo, qg, kg, keys, values, gkeys, gvalues,
    out_ref,
    kbuf, vbuf, gkb, gvb, wbuf, obuf, tok, acc, part_a, part_b, red_a, red_b,
    qf, qa, qb, kn, vn, pa, pb, la, lb, ra, rb, sa, sb, ow, lw, attf, att, msg, rcv, ruler,
    send, single, loc, w_sem, tw_sem, t_sem, r_sem, q_sem, o_sem, ot_sem, p_sem, s_sem, a_sem, m_sem,
):
    nn = 2 * ny
    x = lax.axis_index("prompt")
    n = lax.axis_index("prefix")
    z = lax.axis_index("sample")
    y, c = lax.div(n, 2), lax.rem(n, 2)
    odd = lax.rem(y, 2)
    right, left = lax.rem(x + 1, px), lax.rem(x + px - 1, px)
    across = lax.rem(x + 2, px)
    xodd = lax.rem(x, 2)
    partner = lax.rem(x + 1 + xodd * (px - 2), px)
    other = lax.rem(x + px - 1 - xodd * (px - 2), px)
    rows, width = hid.shape
    batch = keys.shape[0]
    keys_here = keys.shape[1]
    depth = wq.shape[0]
    qcols, kcols = wq.shape[1], wk.shape[1]
    cols = qcols + 2 * kcols
    cut = qcols // 2
    pair = 2 * depth
    window = wbuf.shape[1]
    pad = window - pair
    heads = qcols // 128
    hh = heads // 2
    gr = 8 * hh
    twin = {"prefix": 2 * y + 1 - c}
    peers = [lax.rem(y + i, ny) for i in range(1, ny)]
    others = [{"prefix": 2 * peer + c} for peer in peers]
    beyond = [{"prompt": other, "prefix": 2 * chip + c} for chip in [y] + peers]
    prefix_peers = [lax.rem(n + i, nn) for i in range(1, nn)]
    x_targets = [{"prompt": right}, {"prompt": left}, {"prompt": across}]
    x_sources = [left, right, across]
    per = px * nn // nz

    def home(block, chip):
        return lax.div(block * nn + 2 * chip, per)

    first_chip = lax.div(lax.rem(per * z, nn), 2)

    for i, (src, dst) in enumerate(
        ((keys, kbuf), (values, vbuf), (gkeys, gkb), (gvalues, gvb))
    ):
        pltpu.make_async_copy(src, dst, loc.at[3 + i]).start()
    zero = jnp.zeros((2, pad, cols), wbuf.dtype)
    wbuf[:, 0:pad, :] = zero
    wbuf[:, pair : pair + pad, :] = zero

    barrier = pltpu.get_barrier_semaphore()
    greeted = x_targets + [{"prefix": peer} for peer in prefix_peers] + beyond[1:]
    for device in greeted:
        pl.semaphore_signal(barrier, inc=1, device_id=device, device_id_type=MESH)
    for k in range(2):
        chip = first_chip + k
        for zz in range(nz):

            @pl.when(jnp.logical_or(chip != y, zz != z))
            def _():
                pl.semaphore_signal(
                    barrier,
                    inc=1,
                    device_id={"prefix": 2 * chip + c, "sample": zz},
                    device_id_type=MESH,
                )

    mine_too = jnp.int32(0)
    for block in range(px):
        mine_too = mine_too + (home(block, y) == z).astype(jnp.int32)
    pl.semaphore_wait(barrier, len(greeted) + px * ny - mine_too)

    out = Sends(send, single, ruler)
    base = pl.multiple_of(pad * odd + depth * c, 16)
    mine = pl.ds(base, depth)
    theirs = pl.ds(pl.multiple_of(pad * odd + depth * (1 - c), 16), depth)
    group_a = ((wq.at[:, 0:cut], 0, cut),)
    group_b = (
        (wq.at[:, cut:qcols], cut, qcols - cut),
        (wk, qcols, kcols),
        (wv, qcols + kcols, kcols),
    )
    spans = (slice(0, cut), slice(cut, cols))

    def send_weights(group):
        for piece, lo, size in (group_a, group_b)[group]:
            spot = wbuf.at[1, mine, lo : lo + size]
            out.go(piece, spot, w_sem.at[group], {"prompt": partner})
        for piece, lo, size in (group_a, group_b)[group]:
            spot = wbuf.at[0, mine, lo : lo + size]
            out.go(piece, spot, tw_sem.at[group, 0], twin)
            pltpu.make_async_copy(piece, spot, loc.at[group]).start()

    def start_of(block, chip):
        return pl.multiple_of(128 * lax.div(pair * ny * block + pair * chip, 128), 128)

    send_weights(0)
    blocks = ((x, partner), (other, lax.rem(other + 1 + (1 - xodd) * (px - 2), px)))
    for i in range(2):
        for chip, device in zip([y] + peers, ([None] + others, beyond)[i]):
            for j in range(2):
                piece = hid.at[:, pl.ds(start_of(blocks[i][j], chip), window)]
                spot = tok.at[j, i, y]
                if device is None:
                    pltpu.make_async_copy(piece, spot, t_sem.at[0]).start()
                else:
                    out.go(piece, spot, t_sem.at[0], device)

    send_weights(1)

    def multiply(block, group):
        lhs = tok[block].reshape(2 * ny * rows, window)
        return jnp.dot(
            lhs, wbuf[block, :, spans[group]], preferred_element_type=jnp.float32
        )

    orow = pl.ds(pl.multiple_of(depth * c, 16), depth)
    orow_t = pl.ds(pl.multiple_of(depth * (1 - c), 16), depth)

    def project(group):
        span = spans[group]
        arrived(wbuf.at[1, mine, span], w_sem.at[group])
        out.go(wbuf.at[1, mine, span], wbuf.at[1, mine, span], tw_sem.at[group, 1], twin)
        arrived(wbuf.at[0, mine, span], loc.at[group])
        arrived(wbuf.at[0, theirs, span], tw_sem.at[group, 0])
        if group == 0:
            arrived(tok, t_sem.at[0])
        acc[:, span] = multiply(0, group)
        arrived(wbuf.at[1, theirs, span], tw_sem.at[group, 1])
        part, red = ((part_a, red_a), (part_b, red_b))[group]
        sums = acc[:, span] + multiply(1, group)
        part[...] = sums.astype(part.dtype).reshape(part.shape)
        for peer, device in zip(peers, others):
            out.go(part.at[0, peer], red.at[y], r_sem.at[group], device)
        for chip, device in zip([y] + peers, beyond):
            out.go(part.at[1, chip], red.at[ny + y], r_sem.at[group], device)
        red[y] = part[0, y]

    def gain():
        return qg[...].astype(jnp.float32) * (LOG2E / math.sqrt(128))


    def own(group):
        red = (red_a, red_b)[group]
        arrived(red.at[0 : nn - 1], r_sem.at[group])
        total = red[0].astype(jnp.float32)
        for i in range(1, nn):
            total = total + red[i].astype(jnp.float32)
        for head in range(hh):
            value = norm(total[:, 128 * head : 128 * head + 128], gain())
            for b in range(batch):
                qf[b, 8 * head : 8 * head + 8, :] = value[8 * b : 8 * b + 8]
        q = (qa, qb)[group]
        q[n] = qf[...].astype(q.dtype)
        for peer in prefix_peers:
            out.go(q.at[n], q.at[n], q_sem.at[group], {"prefix": peer})
        return total

    def queries(group):
        q = (qa, qb)[group]
        arrived(q.at[0 : nn - 1], q_sem.at[group])

    def attend(h, group, store_lse):
        for i in range(half):
            b = half * h + i
            q = (qa, qb)[group][:, b].reshape(nn * gr, 128)
            valid = lengths[b] - n * keys_here
            top = total = value = None
            scores = []
            for lo in range(0, keys_here, CHUNK):
                size = min(CHUNK, keys_here - lo)
                k = kbuf[b, lo : lo + size]
                s = lax.dot_general(k, q, NT, preferred_element_type=jnp.float32)
                at = lo + lax.broadcasted_iota(jnp.int32, (size, 1), 0)
                s = s + jnp.where(at < valid, 0.0, -1e30)
                here = jnp.max(s, axis=0, keepdims=True)
                top = here if top is None else jnp.maximum(top, here)
                scores.append(s)
            for s, lo in zip(scores, range(0, keys_here, CHUNK)):
                w = jnp.exp2(s - top)
                add = jnp.sum(w, axis=0, keepdims=True)
                v = vbuf[b, lo : lo + s.shape[0]]
                val = lax.dot_general(
                    v, w.astype(jnp.bfloat16), TN, preferred_element_type=jnp.float32
                )
                total = add if total is None else total + add
                value = val if value is None else value + val
            p = (pa, pb)[group]
            p[:, b] = (value / total).T.astype(p.dtype).reshape(nn, gr, 128)
            store_lse(i, top + jnp.log2(total))

    def attend_own(b):
        q = jnp.concatenate([qa[n, b], qb[n, b]], 0)
        wide = gkb.shape[1]
        s1 = lax.dot_general(q, gkb[b], NT, preferred_element_type=jnp.float32)
        s2 = lax.dot_general(q, kn[b], NT, preferred_element_type=jnp.float32)
        row = lax.rem(lax.broadcasted_iota(jnp.int32, (2 * gr, 1), 0), 8)
        sample, step = lax.div(row, 4), lax.rem(row, 4)
        col = lax.broadcasted_iota(jnp.int32, (1, wide), 1)
        whose = (col >= wide // 2).astype(jnp.int32)
        limit = jnp.where(whose == 0, windows[0, b], windows[1, b] + wide // 2)
        s1 = jnp.where((whose == sample) & (col < limit), s1, -1e30)
        col = lax.broadcasted_iota(jnp.int32, (1, 16), 1)
        s2 = jnp.where((lax.div(col, 4) == sample) & (lax.rem(col, 4) <= step), s2, -1e30)
        top = jnp.maximum(
            jnp.max(s1, axis=-1, keepdims=True), jnp.max(s2, axis=-1, keepdims=True)
        )
        w1 = jnp.exp2(s1 - top)
        w2 = jnp.exp2(s2 - top)
        total = jnp.sum(w1, axis=-1, keepdims=True) + jnp.sum(w2, axis=-1, keepdims=True)
        value = jnp.dot(w1.astype(jnp.bfloat16), gvb[b], preferred_element_type=jnp.float32)
        value = value + jnp.dot(
            w2.astype(jnp.bfloat16), vn[b], preferred_element_type=jnp.float32
        )
        ow[b] = value / total
        lse = top + jnp.log2(total)
        lw[0, pl.ds(b, 1), :] = lanes_of(lse[0:gr], gr)
        lw[1, pl.ds(b, 1), :] = lanes_of(lse[gr:], gr)

    half = batch // 2
    project(0)

    def send_wo():
        for which in range(3):
            out.go(wo, obuf.at[x, orow], o_sem.at[0], x_targets[which])
        out.go(wo, obuf.at[x, orow], ot_sem.at[0], twin)
        pltpu.make_async_copy(wo, obuf.at[x, orow], loc.at[2]).start()

    project(1)
    own(0)
    total = own(1)
    send_wo()
    q_there = qcols - cut
    k_new = norm(total[:, q_there : q_there + kcols], kg[...].astype(jnp.float32))
    v_new = total[:, q_there + kcols :]
    blank = jnp.zeros((8, 128), jnp.float32)
    for b in range(batch):
        kn[b] = jnp.concatenate([k_new[8 * b : 8 * b + 8], blank], 0).astype(kn.dtype)
        vn[b] = jnp.concatenate([v_new[8 * b : 8 * b + 8], blank], 0).astype(vn.dtype)

    arrived(kbuf, loc.at[3])
    arrived(vbuf, loc.at[4])
    queries(0)
    for h in range(2):

        def store_a(i, lse):
            la[half * h + i : half * h + i + 1, :] = lse

        attend(h, 0, store_a)
    for peer in prefix_peers:
        out.go(la, sa.at[n], s_sem.at[0], {"prefix": peer})
        out.go(pa.at[peer], ra.at[n], p_sem.at[0], {"prefix": peer})
    ra[n] = pa[n]
    sa[n] = la[...]

    def attend_b(h):
        def store_b(i, lse):
            lb[h, i : i + 1, :] = lse

        attend(h, 1, store_b)
        span = slice(h * half, h * half + half)
        for peer in prefix_peers:
            device = {"prefix": peer}
            out.go(lb.at[h], sb.at[n, h], s_sem.at[1 + h], device)
            out.go(pb.at[peer, span], rb.at[n, h], p_sem.at[1 + h], device)
        rb[n, h] = pb[n, span]
        sb[n, h] = lb[h]

    row = lax.broadcasted_iota(jnp.int32, (gr, 128), 0)
    lane = lax.broadcasted_iota(jnp.int32, (gr, 128), 1)
    pick = row == lane
    many = nn * gr

    def merge(h):
        if h == 0:
            arrived(sa.at[0 : nn - 1], s_sem.at[0])
            arrived(ra.at[0 : nn - 1], p_sem.at[0])
        arrived(sb.at[0 : nn - 1, h], s_sem.at[1 + h])
        arrived(rb.at[0 : nn - 1, h], p_sem.at[1 + h])
        shift = lax.rem(many - gr * n, many)
        for group in range(2):
            stats = []
            for i in range(nn):
                s = sa[i] if group == 0 else sb[i, h]
                stats.append(pltpu.roll(s, shift, 1)[:, 0:128])
            lo = half * h if group == 0 else 0
            mine_stats = lw[group, half * h : half * h + half, :]
            stats = [s[lo : lo + half] for s in stats] + [mine_stats]
            top = functools.reduce(jnp.maximum, stats)
            parts = [jnp.exp2(s - top) for s in stats]
            inverse = 1.0 / functools.reduce(lambda u, w: u + w, parts)
            parts = [part * inverse for part in parts]
            for i in range(half):
                b = half * h + i
                total = None
                for source in range(nn + 1):
                    weight = jnp.broadcast_to(parts[source][i : i + 1], (gr, 128))
                    weight = jnp.sum(jnp.where(pick, weight, 0.0), axis=-1, keepdims=True)
                    if source == nn:
                        value = ow[b, gr * group : gr * group + gr]
                    elif group == 0:
                        value = ra[source, b].astype(jnp.float32)
                    else:
                        value = rb[source, h, i].astype(jnp.float32)
                    total = weight * value if total is None else total + weight * value
                for head in range(hh):
                    at = 128 * (hh * group + head)
                    attf[8 * i : 8 * i + 8, at : at + 128] = total[8 * head : 8 * head + 8]
        att[h, y] = attf[...].astype(att.dtype)
        for device in others:
            out.go(att.at[h, y], att.at[h, y], a_sem.at[h], device)

    lane8 = lax.broadcasted_iota(jnp.int32, (8, 128), 1)

    def output(h):
        arrived(att.at[h, 0 : ny - 1], a_sem.at[h])
        lhs = att[h].reshape(ny * 16, att.shape[3])
        blank = jnp.zeros((8, 128), jnp.float32)
        for block in range(px):
            main = obuf[block, pl.ds(pl.multiple_of(64 * odd, 64), 256), :]
            rest = obuf[block, pl.ds(pl.multiple_of(256 * (1 - odd), 64), 64), :]
            rest = jnp.concatenate([rest, rest], 0)
            main = lax.dot_general(lhs, main, NT, preferred_element_type=jnp.float32)
            rest = lax.dot_general(lhs, rest, NT, preferred_element_type=jnp.float32)
            for chip in range(ny):
                r = 16 * chip
                msg[h, block, chip, 0:16, :] = main[r : r + 16, 0:128].astype(msg.dtype)
                msg[h, block, chip, 16:32, :] = main[r : r + 16, 128:256].astype(msg.dtype)
                tail = jnp.where(lane8 < 64, rest[r : r + 8], rest[r + 8 : r + 16])
                tail = jnp.concatenate([tail, blank], 0)
                msg[h, block, chip, 32:48, :] = tail.astype(msg.dtype)
            target = home(block, y)
            for i in range(ny):
                chip = lax.rem(y + i, ny)
                out.go(
                    msg.at[h, block, chip],
                    rcv.at[h, odd * nz + z],
                    m_sem.at[h],
                    {"prefix": 2 * chip + c, "sample": target},
                    None if i > 0 else target != z,
                )

            @pl.when(target == z)
            def _():
                rcv[h, odd * nz + z] = msg[h, block, y]

    def collect(h):
        sums = []
        here = jnp.logical_or(first_chip == y, first_chip + 1 == y)

        @pl.when(here)
        def _():
            arrived(rcv.at[h, 0 : 2 * nz - 1], m_sem.at[h])

        @pl.when(jnp.logical_not(here))
        def _():
            arrived(rcv.at[h], m_sem.at[h])

        for k in range(2):
            total = rcv[h, k * nz].astype(jnp.float32)
            for zz in range(1, nz):
                total = total + rcv[h, k * nz + zz].astype(jnp.float32)
            sums.append(total)
        a, d = sums
        u, e = a[32:40], d[32:40]
        low = jnp.where(lane8 < 64, u, pltpu.roll(e, 64, 1))
        high = jnp.where(lane8 < 64, pltpu.roll(u, 64, 1), e)
        middle = jnp.concatenate([low, high], 0)
        tiles = (a[0:16], a[16:32], middle, d[0:16], d[16:32])
        for j, tile in enumerate(tiles):
            tile = tile.astype(out_ref.dtype)
            for i in range(4):
                out_ref[4 * h + i, :, 128 * j : 128 * j + 128] = tile[4 * i : 4 * i + 4]

    queries(1)
    attend_b(0)

    attend_b(1)
    arrived(gkb, loc.at[5])
    arrived(gvb, loc.at[6])

    def own_body(b, _):
        attend_own(b)
        return 0

    lax.fori_loop(0, batch, own_body, 0)
    merge(0)
    arrived(obuf.at[0 : px - 1, orow], o_sem.at[0])
    for source in x_sources:
        spot = obuf.at[source, orow]
        out.go(spot, spot, ot_sem.at[0], twin)
    arrived(obuf.at[x, orow], loc.at[2])
    arrived(obuf.at[:, orow_t], ot_sem.at[0])
    merge(1)
    output(0)
    output(1)
    collect(0)
    collect(1)
    out.finish()


def block_of(px, ny, nz, lengths, windows, hid, wq, wk, wv, wo, qg, kg, keys, values, gk, gv):
    nn = 2 * ny
    rows = hid.shape[0]
    batch = rows // 8
    half = batch // 2
    depth = wq.shape[0]
    qcols = wq.shape[1]
    cols = qcols + 2 * wk.shape[1]
    cut = qcols // 2
    heads = qcols // 128
    gr = 4 * heads
    window = 2 * depth + 64
    any_spec = pl.BlockSpec(memory_space=pl.ANY)
    vmem = pl.BlockSpec(memory_space=pltpu.VMEM)
    smem = pl.BlockSpec(memory_space=pltpu.SMEM)
    dma = pltpu.SemaphoreType.DMA
    bf = jnp.bfloat16
    f32 = jnp.float32
    scratch = [
        (keys.shape, bf),
        (values.shape, bf),
        (gk.shape, bf),
        (gv.shape, bf),
        ((2, window, cols), bf),
        ((px, 2 * depth, wo.shape[1]), bf),
        ((2, 2, ny, rows, window), bf),
        ((2 * ny * rows, cols), f32),
        ((2, ny, rows, cut), bf),
        ((2, ny, rows, cols - cut), bf),
        ((nn, rows, cut), bf),
        ((nn, rows, cols - cut), bf),
        ((batch, gr, 128), f32),
        ((nn, batch, gr, 128), bf),
        ((nn, batch, gr, 128), bf),
        ((batch, 16, 128), bf),
        ((batch, 16, 128), bf),
        ((nn, batch, gr, 128), bf),
        ((nn, batch, gr, 128), bf),
        ((8, nn * gr), f32),
        ((2, 8, nn * gr), f32),
        ((nn, batch, gr, 128), bf),
        ((nn, 2, half, gr, 128), bf),
        ((nn, 8, nn * gr), f32),
        ((nn, 2, 8, nn * gr), f32),
        ((batch, 2 * gr, 128), f32),
        ((2, 8, 128), f32),
        ((16, qcols), f32),
        ((2, ny, 16, qcols), bf),
        ((2, px, ny, 48, 128), bf),
        ((2, 2 * nz, 48, 128), bf),
        ((4096, 128), bf),
    ]
    return pl.pallas_call(
        functools.partial(kernel, px, ny, nz),
        out_shape=jax.ShapeDtypeStruct((rows // 4, 4, 640), bf),
        in_specs=[smem, smem] + [any_spec] * 5 + [vmem] * 2 + [any_spec] * 4,
        out_specs=vmem,
        scratch_shapes=[pltpu.VMEM(shape, dtype) for shape, dtype in scratch]
        + [
            dma((10,)),
            dma((2 * px,)),
            dma((7,)),
            dma((2,)),
            dma((2, 2)),
            dma((1,)),
            dma((2,)),
            dma((2,)),
            dma((1,)),
            dma((1,)),
            dma((3,)),
            dma((3,)),
            dma((2,)),
            dma((2,)),
        ],
        compiler_params=pltpu.CompilerParams(
            collective_id=0, has_side_effects=True, vmem_limit_bytes=60 * 2**20
        ),
        name="block",
    )(lengths, windows, hid, wq, wk, wv, wo, qg, kg, keys, values, gk, gv)


def on_device(
    px, ny, nz,
    new_hidden, query_projection_weight, key_projection_weight, value_projection_weight, w_out,
    query_norm_gain, key_norm_gain, prefix_keys, prompt_cache_values,
    generated_keys, generated_values, prompt_lengths, window_lengths,
):
    batch, samples, steps, width = new_hidden.shape
    dim = query_norm_gain.shape[0]
    block = block_of(
        px,
        ny,
        nz,
        prompt_lengths,
        window_lengths.T,
        new_hidden.reshape(batch * samples * steps, width),
        query_projection_weight,
        key_projection_weight,
        value_projection_weight,
        w_out.T,
        query_norm_gain.reshape(1, dim),
        key_norm_gain.reshape(1, dim),
        prefix_keys.reshape(batch, -1, dim),
        prompt_cache_values.reshape(batch, -1, dim),
        generated_keys.reshape(batch, -1, dim),
        generated_values.reshape(batch, -1, dim),
    )
    return block.reshape(batch, samples, steps, -1)


def solution(mesh):
    sizes = mesh.shape
    body = functools.partial(
        on_device, sizes["prompt"], sizes["prefix"] // 2, sizes["sample"]
    )
    return jax.shard_map(
        body,
        mesh=mesh,
        in_specs=(
            P("prompt", "prefix", None, None),
            P(("prompt", "prefix"), "sample"),
            P(("prompt", "prefix"), "sample"),
            P(("prompt", "prefix"), "sample"),
            P("sample", ("prompt", "prefix")),
            P(),
            P(),
            P("prompt", "prefix", "sample", None),
            P("prompt", "prefix", "sample", None),
            P("prompt", "prefix", None, "sample", None),
            P("prompt", "prefix", None, "sample", None),
            P("prompt"),
            P("prompt", "prefix"),
        ),
        out_specs=P("prompt", "prefix", None, "sample"),
        check_vma=False,
    )
```
